32 devices in a mesh: groups: 2 (over x), dp: 8 (over z, y), tensor: 2 (over core).
Axes of the slice: x: 2, y: 2, z: 4, core: 2. Of those that a mesh axis runs over, the one named last changes fastest.
Arguments:
- train_inputs: bfloat16 [4096, 8192], P(('groups', 'dp'), 'tensor'), parts along dimension 0, as said below
- train_grads: bfloat16 [4096, 28672], P(('groups', 'dp'), 'tensor'), parts along dimension 0, as said below
- proj_in: bfloat16 [8192, 64], P('tensor'), as said below
- proj_out: bfloat16 [28672, 64], P('tensor'), as said below
- queries: bfloat16 [512, 64, 64], P(('groups', 'dp', 'tensor')), parts along dimension 0, may hold values from -6 to 6
Outputs:
- scores: float32 [64, 256], P(('groups', 'dp', 'tensor')), parts along dimension 0
The draws below stay inside these ranges and needn't reach their ends.
There are 2 independent parts, one for each index of `groups`. The reference program is written for one: setup_inputs(seed, part) draws one part's arguments, and reference() takes and returns one part's arrays. A program takes and returns all parts, laid end to end along the dimension named above; an argument that names none is the same for every part. Nothing has to cross between parts.
Inputs may be any that keep to these rules, and one draw needn't show every extreme that they name: `train_inputs`: activations and gradients of order one. `train_grads`: activations and gradients of order one. `proj_in`: factor entries of order 8192 ** -0.5. `proj_out`: factor entries of order 28672 ** -0.5.
All inputs are finite; a program needn't handle non-finite values.
Results may differ from the reference program's by a relative error of at most 0.0065.
The reference program's roundings to bfloat16 on the way (of `grads_proj` and `precond`) count: a program that leaves them out, or rounds other values in their place, can miss the bound.
Values may be sent and summed in bfloat16 or wider, within the bound.
No kernel may reach another device: no remote copies, remote signals or barrier semaphores. Data moves between devices by JAX's collectives and lax.ppermute only.
A program may use at most 64 MiB of HBM per device.

```python
import math
import jax
import jax.numpy as jnp
from jax import lax

D = 8192
FF = 28672
R = 64
SEQ = 64
TRAIN = 32
QUERIES = 256


def shape_rows(key, base):
    rows = base.shape[0]
    cols = base.shape[1]
    key_ex, key_col = jax.random.split(key)
    example = jnp.arange(rows) // SEQ
    spread = jax.random.uniform(key_ex, (TRAIN,), jnp.float32)
    ramp = 1.0 + 2.0 * example.astype(jnp.float32) / max(TRAIN - 1, 1)
    row_scale = ramp * 10.0 ** (0.5 * spread[example]) / 2.5
    col_scale = 10.0 ** jax.random.uniform(key_col, (cols,), jnp.float32) / 4.6
    return base * row_scale[:, None] * col_scale[None, :]


def mixed_factor(key, base, fan_in):
    rank = base.shape[1]
    mixed = base + 0.7 * jnp.roll(base, -1, axis=1)
    col_scale = 2.0 ** jax.random.uniform(key, (rank,), jnp.float32, -1.0, 1.0)
    return mixed * col_scale[None, :] / (1.22 * fan_in ** 0.5)


def draw_train_inputs(key, part):
    key = jax.random.fold_in(key, 11)
    key_base = jax.random.fold_in(key, 0)
    key_scale = jax.random.fold_in(key, 2)
    base = jax.random.normal(key_base, (TRAIN * SEQ, D), jnp.float32)
    return shape_rows(key_scale, base).astype(jnp.bfloat16)


def draw_train_grads(key, part):
    key = jax.random.fold_in(key, 23)
    key_base = jax.random.fold_in(key, 0)
    key_scale = jax.random.fold_in(key, 2)
    base = jax.random.normal(key_base, (TRAIN * SEQ, FF), jnp.float32)
    return shape_rows(key_scale, base).astype(jnp.bfloat16)


def draw_proj_in(key, part):
    key = jax.random.fold_in(key, 37)
    key_base, key_scale = jax.random.split(key)
    base = jax.random.normal(key_base, (D, R), jnp.float32)
    return mixed_factor(key_scale, base, D).astype(jnp.bfloat16)


def draw_proj_out(key, part):
    key = jax.random.fold_in(key, 41)
    key_base, key_scale = jax.random.split(key)
    base = jax.random.normal(key_base, (FF, R), jnp.float32)
    return mixed_factor(key_scale, base, FF).astype(jnp.bfloat16)


def steps_of(rng, dims, cuts, low, high):
    loudness = 1.0
    for dim, parts in cuts:
        heights = jax.random.uniform(jax.random.fold_in(jax.random.fold_in(rng, 6), dim), (parts,), jnp.float32, low / len(cuts), high / len(cuts))
        loudness = loudness * jnp.repeat(jnp.exp(heights), dims[dim] // parts).reshape((-1,) + (1,) * (len(dims) - 1 - dim))
    return loudness


def scatter_about(key, dims, width, limit, pieces=(), kind=jnp.bfloat16):
    values = jax.random.normal(key, dims, jnp.float32) * width
    if len(pieces) > 0:
        values = steps_of(key, dims, pieces, -0.22, 0.18) * values
    return jnp.clip(values, min=-limit, max=limit).astype(kind)


def setup_inputs(seed: int = 0, part: int = 0) -> dict:
    arg_keys = jax.random.split(jax.random.key(seed), 6)
    part_keys = jax.random.split(jax.random.fold_in(arg_keys[5], part), 6)
    train_inputs = draw_train_inputs(jax.random.fold_in(jax.random.fold_in(arg_keys[5], part), 71), part)
    train_grads = draw_train_grads(jax.random.fold_in(jax.random.fold_in(arg_keys[5], part), 71), part)
    proj_in = draw_proj_in(jax.random.fold_in(arg_keys[5], 71), part)
    proj_out = draw_proj_out(jax.random.fold_in(arg_keys[5], 71), part)
    queries = scatter_about(part_keys[4], (QUERIES, R, R), 1.0, 6.0, ((0, 16),))
    return {"train_inputs": train_inputs, "train_grads": train_grads, "proj_in": proj_in, "proj_out": proj_out, "queries": queries}


def damped(cov):
    rank = cov.shape[0]
    shift = 0.1 * jnp.trace(cov) / rank + 1e-06
    return cov + shift * jnp.eye(rank, dtype=jnp.float32)

def precondition(query_f, cov_in, cov_out):
    count = query_f.shape[0]
    rank = query_f.shape[1]
    lower_out = jnp.linalg.cholesky(damped(cov_out))
    lower_in = jnp.linalg.cholesky(damped(cov_in))
    left = query_f.transpose(1, 0, 2).reshape(rank, count * rank)
    middle = jax.scipy.linalg.cho_solve((lower_out, True), left)
    middle_t = middle.reshape(rank, count, rank).transpose(2, 1, 0).reshape(rank, count * rank)
    right = jax.scipy.linalg.cho_solve((lower_in, True), middle_t)
    return right.reshape(rank, count, rank).transpose(1, 2, 0)

def reference(train_inputs, train_grads, proj_in, proj_out, queries):
    acts = jnp.dot(train_inputs.astype(jnp.float32), proj_in.astype(jnp.float32), preferred_element_type=jnp.float32)
    outs = jnp.dot(train_grads.astype(jnp.float32), proj_out.astype(jnp.float32), preferred_element_type=jnp.float32)
    total = acts.shape[0]
    cov_in = jnp.dot(acts.T, acts, precision=lax.Precision.HIGHEST) / total
    cov_out = jnp.dot(outs.T, outs, precision=lax.Precision.HIGHEST) / total
    examples = total // SEQ
    grads_proj = jnp.einsum('esi,esj->eij', outs.reshape(examples, SEQ, R), acts.reshape(examples, SEQ, R), precision=lax.Precision.HIGHEST).astype(jnp.bfloat16)
    precond = precondition(queries.astype(jnp.float32), cov_in, cov_out).astype(jnp.bfloat16)
    score_scale = 1.0 / (math.sqrt(SEQ) * R)
    flat_grads = grads_proj.reshape(examples, R * R)
    flat_query = precond.reshape(queries.shape[0], R * R)
    scores = jnp.einsum('ek,qk->eq', flat_grads.astype(jnp.float32), flat_query.astype(jnp.float32), preferred_element_type=jnp.float32)
    return scores * score_scale
```

```python
import functools
import math

import jax
import jax.numpy as jnp
from jax import lax
from jax.experimental import pallas as pl
from jax.experimental.pallas import tpu as pltpu
from jax.sharding import PartitionSpec as P

SEQ = 64
RANK = 64
WIDE = 4 * RANK
MIB = 1 << 20
F32 = jnp.float32
BF16 = jnp.bfloat16
HBM = pl.BlockSpec(memory_space=pl.ANY)
VMEM = pl.BlockSpec(memory_space=pltpu.VMEM)
SMEM = pl.BlockSpec(memory_space=pltpu.SMEM)


def iota(shape, dim):
    return lax.broadcasted_iota(jnp.int32, shape, dim)


def pieces(x):
    high = x.astype(BF16)
    rest = x - high.astype(F32)
    mid = rest.astype(BF16)
    low = (rest - mid.astype(F32)).astype(BF16)
    return high, mid, low


def dot(a, b):
    return jnp.dot(a, b, preferred_element_type=F32)


def spread_kernel(count, q_ref, out_ref, rows, sems):
    for k in range(q_ref.shape[0]):
        rows[:, k * RANK : (k + 1) * RANK] = q_ref[k]
    copies = [
        pltpu.make_async_copy(rows, out_ref.at[p], sems.at[p]) for p in range(count)
    ]
    for copy in copies:
        copy.start()
    for copy in copies:
        copy.wait()


def spread(queries, count):
    held = queries.shape[0]
    shape = (RANK, held * RANK)
    return pl.pallas_call(
        functools.partial(spread_kernel, count),
        out_shape=jax.ShapeDtypeStruct((count,) + shape, BF16),
        in_specs=[VMEM],
        out_specs=HBM,
        scratch_shapes=[pltpu.VMEM(shape, BF16), pltpu.SemaphoreType.DMA((count,))],
    )(queries)


def project_kernel(
    cuts, x_ref, g_ref, pin_ref, pout_ref, out_ref, x, g, pin, pout, sems
):
    copies = []
    for which, start, size in cuts:
        source, factor, held, held_factor = (
            (x_ref, pin_ref, x, pin) if which == 0 else (g_ref, pout_ref, g, pout)
        )
        here = pl.ds(start, size)
        at = 2 * len(copies)
        pair = (
            pltpu.make_async_copy(
                factor.at[here, :], held_factor.at[here, :], sems.at[at]
            ),
            pltpu.make_async_copy(source.at[:, here], held.at[:, here], sems.at[at + 1]),
        )
        for copy in pair:
            copy.start()
        copies.append(pair)
    totals = [None, None]
    for pair, (which, start, size) in zip(copies, cuts):
        for copy in pair:
            copy.wait()
        here = slice(start, start + size)
        term = dot(x[:, here], pin[here, :]) if which == 0 else dot(g[:, here], pout[here, :])
        totals[which] = term if totals[which] is None else totals[which] + term
    out_ref[:, :RANK] = totals[0]
    out_ref[:, RANK:] = totals[1]


def project(train_inputs, train_grads, proj_in, proj_out):
    tokens = train_inputs.shape[0]
    cuts = []
    for which, array in ((0, train_inputs), (1, train_grads)):
        size = 1024
        cuts += [(which, at, size) for at in range(0, array.shape[1], size)]
    return pl.pallas_call(
        functools.partial(project_kernel, cuts),
        out_shape=jax.ShapeDtypeStruct((tokens, 2 * RANK), F32),
        in_specs=[HBM] * 4,
        out_specs=VMEM,
        scratch_shapes=[
            pltpu.VMEM(train_inputs.shape, BF16),
            pltpu.VMEM(train_grads.shape, BF16),
            pltpu.VMEM(proj_in.shape, BF16),
            pltpu.VMEM(proj_out.shape, BF16),
            pltpu.SemaphoreType.DMA((2 * len(cuts),)),
        ],
        compiler_params=pltpu.CompilerParams(vmem_limit_bytes=40 * MIB),
    )(train_inputs, train_grads, proj_in, proj_out)


def gram_kernel(count, mine_ref, other_ref, cov_ref, grads_ref):
    full = mine_ref[...] + other_ref[...]
    examples = full.shape[0] // SEQ
    total = None
    for e in range(examples):
        rows = full[e * SEQ : (e + 1) * SEQ]
        gram = lax.dot_general(
            rows,
            rows,
            (((0,), (0,)), ((), ())),
            precision=lax.Precision.HIGHEST,
            preferred_element_type=F32,
        )
        grad = gram[RANK:, :RANK].astype(BF16).astype(F32)
        grads_ref[e] = jnp.concatenate([grad, grad], axis=1)
        total = gram if total is None else total + gram
    cov_in = total[:RANK, :RANK]
    cov_out = total[RANK:, RANK:]
    row, col = iota((RANK, RANK), 0), iota((RANK, RANK), 1)
    packed = jnp.where(row >= col, cov_in, cov_out)
    diagonal = jnp.sum(jnp.where(row == col, cov_out, 0.0), axis=0, keepdims=True)
    half = RANK // 2
    body = jnp.concatenate([packed[:half], packed[half:]], axis=1)
    tail = jnp.concatenate([jnp.broadcast_to(diagonal, (8, RANK))] * 2, axis=1)
    for p in range(count):
        cov_ref[p, :half] = body
        cov_ref[p, half:] = tail


def grams(mine, other, count):
    examples = mine.shape[0] // SEQ
    return pl.pallas_call(
        functools.partial(gram_kernel, count),
        out_shape=(
            jax.ShapeDtypeStruct((count, RANK // 2 + 8, 2 * RANK), F32),
            jax.ShapeDtypeStruct((examples, RANK, 2 * RANK), F32),
        ),
        in_specs=[VMEM] * 2,
        out_specs=(VMEM, VMEM),
    )(mine, other)


def inverses(m):
    lane = iota((RANK, 2 * RANK), 1)
    sub = iota((RANK, 2 * RANK), 0)
    left = lane < RANK
    place = jnp.where(left, lane, lane - RANK)
    for k in range(RANK):
        col = jnp.where(left, m[:, k : k + 1], m[:, RANK + k : RANK + k + 1])
        is_col = place == k
        row = jnp.where(is_col[:1], 1.0, m[k : k + 1]) / col[k : k + 1]
        m = jnp.where(sub == k, row, jnp.where(is_col, 0.0, m) - col * row)
    return m


def score_kernel(
    total, held, cov_ref, queries_ref, grads_ref, keep_ref, send_ref, weights, sums
):
    count = cov_ref.shape[0]
    examples = grads_ref.shape[0]
    share = examples // 2
    half = RANK // 2
    core = lax.axis_index("tensor")
    cov = cov_ref[0]
    for p in range(1, count):
        cov = cov + cov_ref[p]
    cov = cov / total
    packed = jnp.concatenate([cov[:half, :RANK], cov[:half, RANK:]], axis=0)
    turned = packed.T
    row, col = iota((RANK, RANK), 0), iota((RANK, RANK), 1)
    cov_in = jnp.where(row >= col, packed, turned)
    cov_out = jnp.where(
        row < col, packed, jnp.where(row == col, cov[half : half + 1, :RANK], turned)
    )

    def damped(c):
        shift = 0.1 * jnp.sum(jnp.where(row == col, c, 0.0)) / RANK + 1e-06
        return jnp.where(row == col, c + shift, c)

    inverse = inverses(jnp.concatenate([damped(cov_in), damped(cov_out)], axis=1))
    inv_in, inv_out = inverse[:, :RANK], inverse[:, RANK:]
    left = jnp.concatenate(pieces(inv_out), axis=0)
    for i, piece in enumerate(pieces(inv_in)):
        weights[i] = jnp.zeros((WIDE, WIDE), BF16)
        for k in range(4):
            here = slice(k * RANK, (k + 1) * RANK)
            weights[i, here, here] = piece
    chunks = held // 4

    def of_peer(p, carry):
        u = dot(left, queries_ref[p])
        y = u[:RANK] + (u[RANK : 2 * RANK] + u[2 * RANK :])
        high, mid, low = pieces(
            jnp.concatenate([y[:, c * WIDE : (c + 1) * WIDE] for c in range(chunks)], axis=0)
        )
        size = chunks * RANK
        by_high = dot(jnp.concatenate([high, mid, low], axis=0), weights[0])
        by_mid = dot(jnp.concatenate([high, mid], axis=0), weights[1])
        by_low = dot(high, weights[2])
        small = by_low + by_mid[size:] + by_high[2 * size :]
        precond = by_high[:size] + (by_high[size : 2 * size] + by_mid[:size] + small)
        precond = precond.astype(BF16).astype(F32)
        for e in range(examples):
            grad = grads_ref[e]
            grad = jnp.concatenate([grad, grad], axis=1)
            for c in range(chunks):
                sums[p, e * chunks + c : e * chunks + c + 1] = jnp.sum(
                    precond[c * RANK : (c + 1) * RANK] * grad, axis=0, keepdims=True
                )
        return carry

    lax.fori_loop(0, count, of_peer, 0)
    width = 2 * held * count
    lanes = (WIDE, width)
    pick = jnp.where(iota(lanes, 0) // RANK == iota(lanes, 1) % 4, 1.0, 0.0).astype(BF16)
    flat = sums[...].reshape(count * examples * chunks, WIDE)
    high, mid, low = pieces(flat)
    found = dot(high, pick) + (dot(mid, pick) + dot(low, pick))
    shape = (count, examples * chunks, width)
    found = found.reshape(shape)
    lane = iota(shape, 2)
    ours = (
        (lane // (2 * held) == iota(shape, 0))
        & ((lane // held) % 2 == core)
        & ((lane % held) // 4 == iota(shape, 1) % chunks)
    )
    found = jnp.sum(jnp.where(ours, found, 0.0), axis=0)
    scale = 1.0 / (math.sqrt(SEQ) * RANK)
    scores = [
        jnp.sum(found[e * chunks : (e + 1) * chunks], axis=0, keepdims=True) * scale
        for e in range(examples)
    ]
    first = jnp.concatenate(scores[:share], axis=0)
    second = jnp.concatenate(scores[share:], axis=0)
    keep_ref[...] = jnp.where(core == 0, first, second)
    send_ref[...] = jnp.where(core == 0, second, first)


def score(cov, queries, grads, total, held):
    count = cov.shape[0]
    examples = grads.shape[0]
    shape = jax.ShapeDtypeStruct((examples // 2, 2 * held * count), F32)
    return pl.pallas_call(
        functools.partial(score_kernel, total, held),
        out_shape=(shape, shape),
        in_specs=[VMEM] * 3,
        out_specs=(VMEM, VMEM),
        scratch_shapes=[
            pltpu.VMEM((3, WIDE, WIDE), BF16),
            pltpu.VMEM((count, examples * (held // 4), WIDE), F32),
        ],
        compiler_params=pltpu.CompilerParams(vmem_limit_bytes=40 * MIB),
    )(cov, queries, grads)


def local(train_inputs, train_grads, proj_in, proj_out, queries):
    count = lax.axis_size("dp")
    swap = [(0, 1), (1, 0)]
    held = queries.shape[0]
    gathered = lax.all_to_all(spread(queries, count), "dp", 0, 0, tiled=True)
    mine = project(train_inputs, train_grads, proj_in, proj_out)
    other = lax.ppermute(mine, "tensor", swap)
    cov, grads = grams(mine, other, count)
    cov = lax.all_to_all(cov, "dp", 0, 0, tiled=True)
    total = train_inputs.shape[0] * count
    keep, send = score(cov, gathered, grads, total, held)
    return keep + lax.ppermute(send, "tensor", swap)


def solution(mesh):
    placed = (
        P(("groups", "dp"), "tensor"),
        P(("groups", "dp"), "tensor"),
        P("tensor", None),
        P("tensor", None),
        P(("groups", "dp", "tensor"), None, None),
    )
    return jax.shard_map(
        local,
        mesh=mesh,
        in_specs=placed,
        out_specs=P(("groups", "dp", "tensor"), None),
        check_vma=False,
    )
```

```python
import functools
import math

import jax
import jax.numpy as jnp
from jax import lax
from jax.experimental import pallas as pl
from jax.experimental.pallas import tpu as pltpu
from jax.sharding import PartitionSpec as P

SEQ = 64
RANK = 64
WIDE = 4 * RANK
MIB = 1 << 20
F32 = jnp.float32
BF16 = jnp.bfloat16
HBM = pl.BlockSpec(memory_space=pl.ANY)
VMEM = pl.BlockSpec(memory_space=pltpu.VMEM)
NT = (((1,), (1,)), ((), ()))


def iota(shape, dim):
    return lax.broadcasted_iota(jnp.int32, shape, dim)


def pieces(x):
    high = x.astype(BF16)
    rest = x - high.astype(F32)
    mid = rest.astype(BF16)
    low = (rest - mid.astype(F32)).astype(BF16)
    return high, mid, low


def dot(a, b):
    return jnp.dot(a, b, preferred_element_type=F32)


def spread_kernel(q_ref, out_ref):
    for k in range(q_ref.shape[0]):
        out_ref[:, k * RANK : (k + 1) * RANK] = q_ref[k]


def spread(queries):
    return pl.pallas_call(
        spread_kernel,
        out_shape=jax.ShapeDtypeStruct((RANK, queries.shape[0] * RANK), BF16),
        in_specs=[VMEM],
        out_specs=VMEM,
    )(queries)


def from_peers(mine, count):
    known = {0: mine}
    bit = count // 2
    while bit:
        pairs = [(i, i ^ bit) for i in range(count)]
        for m in list(known):
            known[m | bit] = lax.ppermute(known[m], "dp", pairs)
        bit //= 2
    return [known[m] for m in range(count)]


def project_kernel(
    cuts, x_ref, g_ref, pin_ref, pout_ref, out_ref, x, g, pin, pout, sems
):
    copies = []
    for which, start, size in cuts:
        source, factor, held, held_factor = (
            (x_ref, pin_ref, x, pin) if which == 0 else (g_ref, pout_ref, g, pout)
        )
        here = pl.ds(start, size)
        at = 2 * len(copies)
        pair = (
            pltpu.make_async_copy(
                factor.at[:, here], held_factor.at[:, here], sems.at[at]
            ),
            pltpu.make_async_copy(source.at[:, here], held.at[:, here], sems.at[at + 1]),
        )
        for copy in pair:
            copy.start()
        copies.append(pair)
    totals = [None, None]
    for pair, (which, start, size) in zip(copies, cuts):
        for copy in pair:
            copy.wait()
        here = slice(start, start + size)
        source, factor = (x, pin) if which == 0 else (g, pout)
        term = lax.dot_general(
            source[:, here], factor[:, here], NT, preferred_element_type=F32
        )
        totals[which] = term if totals[which] is None else totals[which] + term
    out_ref[:, :RANK] = totals[0]
    out_ref[:, RANK:] = totals[1]


def project(train_inputs, train_grads, proj_in, proj_out):
    tokens = train_inputs.shape[0]
    cuts = []
    for which, array in ((0, train_inputs), (1, train_grads)):
        size = 1024
        cuts += [(which, at, size) for at in range(0, array.shape[1], size)]
    return pl.pallas_call(
        functools.partial(project_kernel, cuts),
        out_shape=jax.ShapeDtypeStruct((tokens, 2 * RANK), F32),
        in_specs=[HBM] * 4,
        out_specs=VMEM,
        scratch_shapes=[
            pltpu.VMEM(train_inputs.shape, BF16),
            pltpu.VMEM(train_grads.shape, BF16),
            pltpu.VMEM(proj_in.shape[::-1], BF16),
            pltpu.VMEM(proj_out.shape[::-1], BF16),
            pltpu.SemaphoreType.DMA((2 * len(cuts),)),
        ],
        compiler_params=pltpu.CompilerParams(vmem_limit_bytes=60 * MIB),
    )(train_inputs, train_grads, proj_in.T, proj_out.T)


def gram_kernel(count, mine_ref, other_ref, cov_ref, grads_ref):
    full = mine_ref[...] + other_ref[...]
    examples = full.shape[0] // SEQ
    total = None
    for e in range(examples):
        rows = full[e * SEQ : (e + 1) * SEQ]
        gram = lax.dot_general(
            rows,
            rows,
            (((0,), (0,)), ((), ())),
            precision=lax.Precision.HIGHEST,
            preferred_element_type=F32,
        )
        grad = gram[RANK:, :RANK].astype(BF16).astype(F32)
        grads_ref[e] = jnp.concatenate([grad, grad], axis=1)
        total = gram if total is None else total + gram
    cov_in = total[:RANK, :RANK]
    cov_out = total[RANK:, RANK:]
    row, col = iota((RANK, RANK), 0), iota((RANK, RANK), 1)
    packed = jnp.where(row >= col, cov_in, cov_out)
    diagonal = jnp.sum(jnp.where(row == col, cov_out, 0.0), axis=0, keepdims=True)
    half = RANK // 2
    body = jnp.concatenate([packed[:half], packed[half:]], axis=1)
    tail = jnp.concatenate([jnp.broadcast_to(diagonal, (8, RANK))] * 2, axis=1)
    for p in range(count):
        cov_ref[p, :half] = body
        cov_ref[p, half:] = tail


def grams(mine, other, count):
    examples = mine.shape[0] // SEQ
    return pl.pallas_call(
        functools.partial(gram_kernel, count),
        out_shape=(
            jax.ShapeDtypeStruct((count, RANK // 2 + 8, 2 * RANK), F32),
            jax.ShapeDtypeStruct((examples, RANK, 2 * RANK), F32),
        ),
        in_specs=[VMEM] * 2,
        out_specs=(VMEM, VMEM),
    )(mine, other)


def inverses(m):
    lane = iota((RANK, 2 * RANK), 1)
    sub = iota((RANK, 2 * RANK), 0)
    left = lane < RANK
    place = jnp.where(left, lane, lane - RANK)
    for k in range(RANK):
        col = jnp.where(left, m[:, k : k + 1], m[:, RANK + k : RANK + k + 1])
        is_col = place == k
        row = jnp.where(is_col[:1], 1.0, m[k : k + 1]) / col[k : k + 1]
        m = jnp.where(sub == k, row, jnp.where(is_col, 0.0, m) - col * row)
    return m


def score_kernel(
    total, held, count, cov_ref, grads_ref, *rest
):
    queries_refs = rest[:count]
    keep_ref, send_ref, queries, weights, sums = rest[count:]
    for p in range(count):
        queries[p] = queries_refs[p][...]
    examples = grads_ref.shape[0]
    share = examples // 2
    half = RANK // 2
    core = lax.axis_index("tensor")
    cov = cov_ref[0]
    for p in range(1, count):
        cov = cov + cov_ref[p]
    cov = cov / total
    packed = jnp.concatenate([cov[:half, :RANK], cov[:half, RANK:]], axis=0)
    turned = packed.T
    row, col = iota((RANK, RANK), 0), iota((RANK, RANK), 1)
    cov_in = jnp.where(row >= col, packed, turned)
    cov_out = jnp.where(
        row < col, packed, jnp.where(row == col, cov[half : half + 1, :RANK], turned)
    )

    def damped(c):
        shift = 0.1 * jnp.sum(jnp.where(row == col, c, 0.0)) / RANK + 1e-06
        return jnp.where(row == col, c + shift, c)

    inverse = inverses(jnp.concatenate([damped(cov_in), damped(cov_out)], axis=1))
    inv_in, inv_out = inverse[:, :RANK], inverse[:, RANK:]
    left = jnp.concatenate(pieces(inv_out), axis=0)
    for i, piece in enumerate(pieces(inv_in)):
        weights[i] = jnp.zeros((WIDE, WIDE), BF16)
        for k in range(4):
            here = slice(k * RANK, (k + 1) * RANK)
            weights[i, here, here] = piece
    chunks = held // 4

    def of_peer(p, carry):
        u = dot(left, queries[p])
        y = u[:RANK] + (u[RANK : 2 * RANK] + u[2 * RANK :])
        high, mid, low = pieces(
            jnp.concatenate([y[:, c * WIDE : (c + 1) * WIDE] for c in range(chunks)], axis=0)
        )
        size = chunks * RANK
        by_high = dot(jnp.concatenate([high, mid, low], axis=0), weights[0])
        by_mid = dot(jnp.concatenate([high, mid], axis=0), weights[1])
        by_low = dot(high, weights[2])
        small = by_low + by_mid[size:] + by_high[2 * size :]
        precond = by_high[:size] + (by_high[size : 2 * size] + by_mid[:size] + small)
        precond = precond.astype(BF16).astype(F32)
        for e in range(examples):
            grad = grads_ref[e]
            grad = jnp.concatenate([grad, grad], axis=1)
            for c in range(chunks):
                sums[p, e * chunks + c : e * chunks + c + 1] = jnp.sum(
                    precond[c * RANK : (c + 1) * RANK] * grad, axis=0, keepdims=True
                )
        return carry

    lax.fori_loop(0, count, of_peer, 0)
    width = 2 * held * count
    lanes = (WIDE, width)
    pick = jnp.where(iota(lanes, 0) // RANK == iota(lanes, 1) % 4, 1.0, 0.0).astype(BF16)
    flat = sums[...].reshape(count * examples * chunks, WIDE)
    high, mid, low = pieces(flat)
    found = dot(high, pick) + (dot(mid, pick) + dot(low, pick))
    shape = (count, examples * chunks, width)
    found = found.reshape(shape)
    lane = iota(shape, 2)
    ours = (
        (lane // (2 * held) == (iota(shape, 0) ^ lax.axis_index("dp")))
        & ((lane // held) % 2 == core)
        & ((lane % held) // 4 == iota(shape, 1) % chunks)
    )
    found = jnp.sum(jnp.where(ours, found, 0.0), axis=0)
    scale = 1.0 / (math.sqrt(SEQ) * RANK)
    scores = [
        jnp.sum(found[e * chunks : (e + 1) * chunks], axis=0, keepdims=True) * scale
        for e in range(examples)
    ]
    first = jnp.concatenate(scores[:share], axis=0)
    second = jnp.concatenate(scores[share:], axis=0)
    keep_ref[...] = jnp.where(core == 0, first, second)
    send_ref[...] = jnp.where(core == 0, second, first)


def score(cov, queries, grads, total, held):
    count = cov.shape[0]
    examples = grads.shape[0]
    queries_shape = (count,) + queries[0].shape
    shape = jax.ShapeDtypeStruct((examples // 2, 2 * held * count), F32)
    return pl.pallas_call(
        functools.partial(score_kernel, total, held, count),
        out_shape=(shape, shape),
        in_specs=[VMEM] * (2 + count),
        out_specs=(VMEM, VMEM),
        scratch_shapes=[
            pltpu.VMEM(queries_shape, BF16),
            pltpu.VMEM((3, WIDE, WIDE), BF16),
            pltpu.VMEM((count, examples * (held // 4), WIDE), F32),
        ],
        compiler_params=pltpu.CompilerParams(vmem_limit_bytes=40 * MIB),
    )(cov, grads, *queries)


def local(train_inputs, train_grads, proj_in, proj_out, queries):
    count = lax.axis_size("dp")
    swap = [(0, 1), (1, 0)]
    held = queries.shape[0]
    gathered = from_peers(spread(queries), count)
    mine = project(train_inputs, train_grads, proj_in, proj_out)
    other = lax.ppermute(mine, "tensor", swap)
    cov, grads = grams(mine, other, count)
    cov = lax.all_to_all(cov, "dp", 0, 0, tiled=True)
    total = train_inputs.shape[0] * count
    keep, send = score(cov, gathered, grads, total, held)
    return keep + lax.ppermute(send, "tensor", swap)


def solution(mesh):
    placed = (
        P(("groups", "dp"), "tensor"),
        P(("groups", "dp"), "tensor"),
        P("tensor", None),
        P("tensor", None),
        P(("groups", "dp", "tensor"), None, None),
    )
    return jax.shard_map(
        local,
        mesh=mesh,
        in_specs=placed,
        out_specs=P(("groups", "dp", "tensor"), None),
        check_vma=False,
    )
```

```python
import functools
import math

import jax
import jax.numpy as jnp
from jax import lax
from jax.experimental import pallas as pl
from jax.experimental.pallas import tpu as pltpu
from jax.sharding import PartitionSpec as P

SEQ = 64
RANK = 64
WIDE = 4 * RANK
MIB = 1 << 20
F32 = jnp.float32
BF16 = jnp.bfloat16
HBM = pl.BlockSpec(memory_space=pl.ANY)
VMEM = pl.BlockSpec(memory_space=pltpu.VMEM)


def cost(us):
    return pl.CostEstimate(flops=0, bytes_accessed=int(us * 3.7e6), transcendentals=0)


NT = (((1,), (1,)), ((), ()))


SMALL = pltpu.CompilerParams(vmem_limit_bytes=4 * MIB)


def iota(shape, dim):
    return lax.broadcasted_iota(jnp.int32, shape, dim)


def pieces(x):
    high = x.astype(BF16)
    rest = x - high.astype(F32)
    mid = rest.astype(BF16)
    low = (rest - mid.astype(F32)).astype(BF16)
    return high, mid, low


def dot(a, b):
    return jnp.dot(a, b, preferred_element_type=F32)


def spread_kernel(q_ref, out_ref):
    for k in range(q_ref.shape[0]):
        out_ref[:, k * RANK : (k + 1) * RANK] = q_ref[k]


def spread(queries):
    return pl.pallas_call(
        spread_kernel,
        out_shape=jax.ShapeDtypeStruct((RANK, queries.shape[0] * RANK), BF16),
        cost_estimate=cost(2),
        in_specs=[VMEM],
        out_specs=VMEM,
        compiler_params=SMALL,
    )(queries)


def flips(count):
    return list(range(0, count, 2))


def flipped(x, count, flip):
    return lax.ppermute(x, "dp", [(i, i ^ flip) for i in range(count)])


def from_peers(mine, count):
    known = {0: mine}
    bit = count // 2
    while bit > 1:
        for m in list(known):
            known[m | bit] = flipped(known[m], count, bit)
        bit //= 2
    return [known[m] for m in flips(count)]


def project_kernel(
    cuts, x_ref, g_ref, pin_ref, pout_ref, after_ref, first_ref, second_ref, x, g, pin, pout, sems
):
    copies = []
    for which, start, size in cuts:
        source, factor, held, held_factor = (
            (x_ref, pin_ref, x, pin) if which == 0 else (g_ref, pout_ref, g, pout)
        )
        here = pl.ds(start, size)
        at = 2 * len(copies)
        pair = (
            pltpu.make_async_copy(
                factor.at[:, here], held_factor.at[:, here], sems.at[at]
            ),
            pltpu.make_async_copy(source.at[:, here], held.at[:, here], sems.at[at + 1]),
        )
        for copy in pair:
            copy.start()
        copies.append(pair)
    totals = [None, None]
    for pair, (which, start, size) in zip(copies, cuts):
        for copy in pair:
            copy.wait()
        here = slice(start, start + size)
        source, factor = (x, pin) if which == 0 else (g, pout)
        term = lax.dot_general(
            source[:, here], factor[:, here], NT, preferred_element_type=F32
        )
        totals[which] = term if totals[which] is None else totals[which] + term
    half = totals[0].shape[0] // 2
    for part, out_ref in enumerate((first_ref, second_ref)):
        here = slice(part * half, (part + 1) * half)
        out_ref[:, :RANK] = totals[0][here]
        out_ref[:, RANK:] = totals[1][here]


def project(train_inputs, train_grads, proj_in, proj_out, after):
    half = jax.ShapeDtypeStruct((train_inputs.shape[0] // 2, 2 * RANK), F32)
    cuts = []
    for which, array in ((0, train_inputs), (1, train_grads)):
        size = 1024
        cuts += [(which, at, size) for at in range(0, array.shape[1], size)]
    return pl.pallas_call(
        functools.partial(project_kernel, cuts),
        out_shape=(half, half),
        cost_estimate=cost(8),
        in_specs=[HBM] * 5,
        out_specs=(VMEM, VMEM),
        scratch_shapes=[
            pltpu.VMEM(train_inputs.shape, BF16),
            pltpu.VMEM(train_grads.shape, BF16),
            pltpu.VMEM(proj_in.shape[::-1], BF16),
            pltpu.VMEM(proj_out.shape[::-1], BF16),
            pltpu.SemaphoreType.DMA((2 * len(cuts),)),
        ],
        compiler_params=pltpu.CompilerParams(vmem_limit_bytes=58 * MIB),
    )(train_inputs, train_grads, proj_in.T, proj_out.T, after)


def over_rows(a):
    return lax.dot_general(
        a,
        a,
        (((0,), (0,)), ((), ())),
        precision=lax.Precision.HIGHEST,
        preferred_element_type=F32,
    )


def both_halves(refs):
    a, b, c, d = refs
    return jnp.concatenate([a[...] + c[...], b[...] + d[...]], axis=0)


def covariance_kernel(count, *refs):
    cov_ref = refs[-1]
    gram = over_rows(both_halves(refs[:4]))
    cov_in = gram[:RANK, :RANK]
    cov_out = gram[RANK:, RANK:]
    row, col = iota((RANK, RANK), 0), iota((RANK, RANK), 1)
    packed = jnp.where(row >= col, cov_in, cov_out)
    diagonal = jnp.sum(jnp.where(row == col, cov_out, 0.0), axis=0, keepdims=True)
    half = RANK // 2
    body = jnp.concatenate([packed[:half], packed[half:]], axis=1)
    tail = jnp.concatenate([jnp.broadcast_to(diagonal, (8, RANK))] * 2, axis=1)
    for p in range(count):
        cov_ref[p, :half] = body
        cov_ref[p, half:] = tail


def covariances(mine, other, after, count):
    return pl.pallas_call(
        functools.partial(covariance_kernel, count),
        out_shape=jax.ShapeDtypeStruct((count, RANK // 2 + 8, 2 * RANK), F32),
        cost_estimate=cost(2),
        in_specs=[VMEM] * (4 + len(after)),
        out_specs=VMEM,
        compiler_params=SMALL,
    )(*mine, *other, *after)


def gradient_kernel(*refs):
    grads_ref = refs[-1]
    full = both_halves(refs[:4])
    for e in range(full.shape[0] // SEQ):
        gram = over_rows(full[e * SEQ : (e + 1) * SEQ])
        grads_ref[:, e * RANK : (e + 1) * RANK] = gram[RANK:, :RANK].astype(BF16)


def gradients(mine, other):
    examples = 2 * mine[0].shape[0] // SEQ
    return pl.pallas_call(
        gradient_kernel,
        out_shape=jax.ShapeDtypeStruct((RANK, examples * RANK), BF16),
        cost_estimate=cost(2),
        in_specs=[VMEM] * 4,
        out_specs=VMEM,
        compiler_params=SMALL,
    )(*mine, *other)


def inverse_2(m):
    a, b, c, d = m
    scale = 1.0 / (a * d - b * c)
    return d * scale, -b * scale, -c * scale, a * scale


def times_2(m, n):
    a, b, c, d = m
    e, f, g, h = n
    return a * e + b * g, a * f + b * h, c * e + d * g, c * f + d * h


def minus_2(m, n):
    return tuple(i - j for i, j in zip(m, n))


def inverse_4(entry):
    block = lambda i, j: (
        entry(i, j),
        entry(i, j + 1),
        entry(i + 1, j),
        entry(i + 1, j + 1),
    )
    b, c = block(0, 2), block(2, 0)
    first = inverse_2(block(0, 0))
    first_b, c_first = times_2(first, b), times_2(c, first)
    last = inverse_2(minus_2(block(2, 2), times_2(c, first_b)))
    upper = tuple(-i for i in times_2(first_b, last))
    lower = tuple(-i for i in times_2(last, c_first))
    first = minus_2(first, times_2(upper, c_first))
    return (
        (first[0], first[1], upper[0], upper[1]),
        (first[2], first[3], upper[2], upper[3]),
        (lower[0], lower[1], last[0], last[1]),
        (lower[2], lower[3], last[2], last[3]),
    )


def inverses(m):
    lane = iota((RANK, 2 * RANK), 1)
    sub = iota((RANK, 2 * RANK), 0)
    left = lane < RANK
    place = jnp.where(left, lane, lane - RANK)
    for k in range(0, RANK, 4):
        cols = [
            jnp.where(left, m[:, k + i : k + i + 1], m[:, RANK + k + i : RANK + k + i + 1])
            for i in range(4)
        ]
        pivot = inverse_4(lambda i, j: cols[j][k + i : k + i + 1])
        rows = []
        for i in range(4):
            row = m[k + i : k + i + 1]
            for j in range(4):
                row = jnp.where(place[:1] == k + j, 1.0 if i == j else 0.0, row)
            rows.append(row)
        news = [
            (p[0] * rows[0] + p[1] * rows[1]) + (p[2] * rows[2] + p[3] * rows[3])
            for p in pivot
        ]
        m = jnp.where((place >= k) & (place < k + 4), 0.0, m)
        m = (m - cols[0] * news[0] - cols[1] * news[1]) - (
            cols[2] * news[2] + cols[3] * news[3]
        )
        for i in range(4):
            m = jnp.where(sub == k + i, news[i], m)
    return m


def score_kernel(total, held, count, cov_ref, *rest):
    peers = len(flips(count))
    grads_refs, rest = rest[:2], rest[2:]
    queries_refs, rest = rest[:peers], rest[peers:]
    out_refs, (queries, weights, sums) = rest[:4], rest[4:]
    for p in range(peers):
        queries[p] = queries_refs[p][...]
    examples = 2 * grads_refs[0].shape[1] // RANK
    half = RANK // 2
    core = lax.axis_index("tensor")
    cov = cov_ref[0]
    for p in range(1, count):
        cov = cov + cov_ref[p]
    cov = cov / total
    packed = jnp.concatenate([cov[:half, :RANK], cov[:half, RANK:]], axis=0)
    turned = packed.T
    row, col = iota((RANK, RANK), 0), iota((RANK, RANK), 1)
    cov_in = jnp.where(row >= col, packed, turned)
    cov_out = jnp.where(
        row < col, packed, jnp.where(row == col, cov[half : half + 1, :RANK], turned)
    )

    def damped(c):
        shift = 0.1 * jnp.sum(jnp.where(row == col, c, 0.0)) / RANK + 1e-06
        return jnp.where(row == col, c + shift, c)

    inverse = inverses(jnp.concatenate([damped(cov_in), damped(cov_out)], axis=1))
    inv_in, inv_out = inverse[:, :RANK], inverse[:, RANK:]
    left = jnp.concatenate(pieces(inv_out), axis=0)
    for i, piece in enumerate(pieces(inv_in)):
        weights[i] = jnp.zeros((WIDE, WIDE), BF16)
        for k in range(4):
            here = slice(k * RANK, (k + 1) * RANK)
            weights[i, here, here] = piece
    chunks = held // 4
    grads = []
    for ref in grads_refs:
        both = ref[...].astype(F32)
        for e in range(examples // 2):
            grad = both[:, e * RANK : (e + 1) * RANK]
            grads.append(jnp.concatenate([grad] * 4, axis=1))

    def of_peer(p, carry):
        u = dot(left, queries[p])
        y = u[:RANK] + (u[RANK : 2 * RANK] + u[2 * RANK :])
        high, mid, low = pieces(
            jnp.concatenate([y[:, c * WIDE : (c + 1) * WIDE] for c in range(chunks)], axis=0)
        )
        size = chunks * RANK
        by_high = dot(jnp.concatenate([high, mid, low], axis=0), weights[0])
        by_mid = dot(jnp.concatenate([high, mid], axis=0), weights[1])
        by_low = dot(high, weights[2])
        small = by_low + by_mid[size:] + by_high[2 * size :]
        precond = by_high[:size] + (by_high[size : 2 * size] + by_mid[:size] + small)
        precond = precond.astype(BF16).astype(F32)
        for e in range(examples):
            for c in range(chunks):
                sums[p, e * chunks + c : e * chunks + c + 1] = jnp.sum(
                    precond[c * RANK : (c + 1) * RANK] * grads[e], axis=0, keepdims=True
                )
        return carry

    lax.fori_loop(0, peers, of_peer, 0)
    width = 2 * held * count
    lanes = (WIDE, width)
    pick = jnp.where(iota(lanes, 0) // RANK == iota(lanes, 1) % 4, 1.0, 0.0).astype(BF16)
    flat = sums[...].reshape(peers * examples * chunks, WIDE)
    high, mid, low = pieces(flat)
    found = dot(high, pick) + (dot(mid, pick) + dot(low, pick))
    shape = (peers, examples * chunks, width)
    found = found.reshape(shape)
    lane = iota(shape, 2)
    ours = (
        (lane // (2 * held) == ((2 * iota(shape, 0)) ^ lax.axis_index("dp")))
        & ((lane // held) % 2 == core)
        & ((lane % held) // 4 == iota(shape, 1) % chunks)
    )
    found = jnp.sum(jnp.where(ours, found, 0.0), axis=0)
    scale = 1.0 / (math.sqrt(SEQ) * RANK)
    scores = [
        jnp.sum(found[e * chunks : (e + 1) * chunks], axis=0, keepdims=True) * scale
        for e in range(examples)
    ]
    share = examples // 4
    blocks = [
        jnp.concatenate(scores[i * share : (i + 1) * share], axis=0) for i in range(4)
    ]
    for i in (0, 2):
        out_refs[i][...] = jnp.where(core == 0, blocks[i], blocks[i + 1])
        out_refs[i + 1][...] = jnp.where(core == 0, blocks[i + 1], blocks[i])


def score(cov, grads, queries, total, held):
    count = cov.shape[0]
    peers = len(queries)
    examples = 2 * grads[0].shape[1] // RANK
    shape = jax.ShapeDtypeStruct((examples // 4, 2 * held * count), F32)
    return pl.pallas_call(
        functools.partial(score_kernel, total, held, count),
        out_shape=(shape,) * 4,
        cost_estimate=cost(10),
        in_specs=[VMEM] * (3 + peers),
        out_specs=(VMEM,) * 4,
        scratch_shapes=[
            pltpu.VMEM((peers,) + queries[0].shape, BF16),
            pltpu.VMEM((3, WIDE, WIDE), BF16),
            pltpu.VMEM((peers, examples * (held // 4), WIDE), F32),
        ],
        compiler_params=pltpu.CompilerParams(vmem_limit_bytes=24 * MIB),
    )(cov, *grads, *queries)


def local(train_inputs, train_grads, proj_in, proj_out, queries):
    count = lax.axis_size("dp")
    swap = [(0, 1), (1, 0)]
    held = queries.shape[0]
    spread_queries = spread(queries)
    gathered = from_peers(spread_queries, count)
    mine = project(train_inputs, train_grads, proj_in, proj_out, spread_queries)
    other = [lax.ppermute(part, "tensor", swap) for part in mine]
    cov = covariances(mine, other, [gathered[count // 4]], count)
    cov = lax.all_to_all(cov, "dp", 0, 0, tiled=True)
    grads = gradients(mine, other)
    total = train_inputs.shape[0] * count
    pair = (grads, flipped(grads, count, 1))
    keep, to_core, to_chip, to_far = score(cov, pair, gathered, total, held)
    corner = [(i, i ^ 3) for i in range(2 * count)]
    return (
        (keep + lax.ppermute(to_core, "tensor", swap))
        + (flipped(to_chip, count, 1) + lax.ppermute(to_far, ("dp", "tensor"), corner))
    )


def solution(mesh):
    placed = (
        P(("groups", "dp"), "tensor"),
        P(("groups", "dp"), "tensor"),
        P("tensor", None),
        P("tensor", None),
        P(("groups", "dp", "tensor"), None, None),
    )
    return jax.shard_map(
        local,
        mesh=mesh,
        in_specs=placed,
        out_specs=P(("groups", "dp", "tensor"), None),
        check_vma=False,
    )
```

```python
import functools
import math

import jax
import jax.numpy as jnp
from jax import lax
from jax.experimental import pallas as pl
from jax.experimental.pallas import tpu as pltpu
from jax.sharding import PartitionSpec as P

SEQ = 64
RANK = 64
WIDE = 4 * RANK
MIB = 1 << 20
F32 = jnp.float32
BF16 = jnp.bfloat16
HBM = pl.BlockSpec(memory_space=pl.ANY)
VMEM = pl.BlockSpec(memory_space=pltpu.VMEM)


def cost(us):
    return pl.CostEstimate(flops=0, bytes_accessed=int(us * 3.7e6), transcendentals=0)


NT = (((1,), (1,)), ((), ()))


SMALL = pltpu.CompilerParams(vmem_limit_bytes=4 * MIB)


def iota(shape, dim):
    return lax.broadcasted_iota(jnp.int32, shape, dim)


def pieces(x):
    high = x.astype(BF16)
    rest = x - high.astype(F32)
    mid = rest.astype(BF16)
    low = (rest - mid.astype(F32)).astype(BF16)
    return high, mid, low


def dot(a, b):
    return jnp.dot(a, b, preferred_element_type=F32)


def spread_kernel(q_ref, out_ref):
    for k in range(q_ref.shape[0]):
        out_ref[:, k * RANK : (k + 1) * RANK] = q_ref[k]


def spread(queries):
    return pl.pallas_call(
        spread_kernel,
        out_shape=jax.ShapeDtypeStruct((RANK, queries.shape[0] * RANK), BF16),
        cost_estimate=cost(2),
        in_specs=[VMEM],
        out_specs=VMEM,
        compiler_params=SMALL,
    )(queries)


def flips(count):
    return list(range(0, count, 2))


def flipped(x, count, flip):
    return lax.ppermute(x, "dp", [(i, i ^ flip) for i in range(count)])


def from_peers(mine, count):
    known = {0: mine}
    bits = []
    while 2 << len(bits) < count:
        bits.append(2 << len(bits))
    for bit in reversed(bits[-2:]):
        known[bit] = flipped(mine, count, bit)
    for i, bit in enumerate(reversed(bits)):
        for m in sorted(known):
            if m & bit == 0 and m | bit not in known and m % (2 * bit) == 0:
                known[m | bit] = flipped(known[m], count, bit)
    return [known[m] for m in flips(count)]


def project_kernel(
    cuts, x_ref, g_ref, pin_ref, pout_ref, after_ref, first_ref, second_ref, x, g, pin, pout, sems
):
    copies = []
    for which, start, size in cuts:
        source, factor, held, held_factor = (
            (x_ref, pin_ref, x, pin) if which == 0 else (g_ref, pout_ref, g, pout)
        )
        here = pl.ds(start, size)
        at = 2 * len(copies)
        pair = (
            pltpu.make_async_copy(
                factor.at[:, here], held_factor.at[:, here], sems.at[at]
            ),
            pltpu.make_async_copy(source.at[:, here], held.at[:, here], sems.at[at + 1]),
        )
        for copy in pair:
            copy.start()
        copies.append(pair)
    totals = [None, None]
    for pair, (which, start, size) in zip(copies, cuts):
        for copy in pair:
            copy.wait()
        here = slice(start, start + size)
        source, factor = (x, pin) if which == 0 else (g, pout)
        term = lax.dot_general(
            source[:, here], factor[:, here], NT, preferred_element_type=F32
        )
        totals[which] = term if totals[which] is None else totals[which] + term
    half = totals[0].shape[0] // 2
    for part, out_ref in enumerate((first_ref, second_ref)):
        here = slice(part * half, (part + 1) * half)
        out_ref[:, :RANK] = totals[0][here]
        out_ref[:, RANK:] = totals[1][here]


def project(train_inputs, train_grads, proj_in, proj_out, after):
    half = jax.ShapeDtypeStruct((train_inputs.shape[0] // 2, 2 * RANK), F32)
    cuts = []
    for which, array in ((0, train_inputs), (1, train_grads)):
        size = 1024
        cuts += [(which, at, size) for at in range(0, array.shape[1], size)]
    return pl.pallas_call(
        functools.partial(project_kernel, cuts),
        out_shape=(half, half),
        cost_estimate=cost(8),
        in_specs=[HBM] * 5,
        out_specs=(VMEM, VMEM),
        scratch_shapes=[
            pltpu.VMEM(train_inputs.shape, BF16),
            pltpu.VMEM(train_grads.shape, BF16),
            pltpu.VMEM(proj_in.shape[::-1], BF16),
            pltpu.VMEM(proj_out.shape[::-1], BF16),
            pltpu.SemaphoreType.DMA((2 * len(cuts),)),
        ],
        compiler_params=pltpu.CompilerParams(vmem_limit_bytes=107 * MIB // 2),
    )(train_inputs, train_grads, proj_in.T, proj_out.T, after)


def over_rows(a):
    return lax.dot_general(
        a,
        a,
        (((0,), (0,)), ((), ())),
        precision=lax.Precision.HIGHEST,
        preferred_element_type=F32,
    )


def both_halves(refs):
    a, b, c, d = refs
    return jnp.concatenate([a[...] + c[...], b[...] + d[...]], axis=0)


def covariance_kernel(count, *refs):
    cov_ref = refs[-1]
    gram = over_rows(both_halves(refs[:4]))
    cov_in = gram[:RANK, :RANK]
    cov_out = gram[RANK:, RANK:]
    row, col = iota((RANK, RANK), 0), iota((RANK, RANK), 1)
    packed = jnp.where(row >= col, cov_in, cov_out)
    diagonal = jnp.sum(jnp.where(row == col, cov_out, 0.0), axis=0, keepdims=True)
    half = RANK // 2
    body = jnp.concatenate([packed[:half], packed[half:]], axis=1)
    tail = jnp.concatenate([jnp.broadcast_to(diagonal, (8, RANK))] * 2, axis=1)
    for p in range(count):
        cov_ref[p, :half] = body
        cov_ref[p, half:] = tail


def covariances(mine, other, after, count):
    return pl.pallas_call(
        functools.partial(covariance_kernel, count),
        out_shape=jax.ShapeDtypeStruct((count, RANK // 2 + 8, 2 * RANK), F32),
        cost_estimate=cost(2),
        in_specs=[VMEM] * (4 + len(after)),
        out_specs=VMEM,
        compiler_params=SMALL,
    )(*mine, *other, *after)


def gradient_kernel(*refs):
    grads_ref = refs[-1]
    full = both_halves(refs[:4])
    for e in range(full.shape[0] // SEQ):
        gram = over_rows(full[e * SEQ : (e + 1) * SEQ])
        grads_ref[:, e * RANK : (e + 1) * RANK] = gram[RANK:, :RANK].astype(BF16)


def gradients(mine, other):
    examples = 2 * mine[0].shape[0] // SEQ
    return pl.pallas_call(
        gradient_kernel,
        out_shape=jax.ShapeDtypeStruct((RANK, examples * RANK), BF16),
        cost_estimate=cost(2),
        in_specs=[VMEM] * 4,
        out_specs=VMEM,
        compiler_params=SMALL,
    )(*mine, *other)


def inverse_2(m):
    a, b, c, d = m
    scale = 1.0 / (a * d - b * c)
    return d * scale, -b * scale, -c * scale, a * scale


def times_2(m, n):
    a, b, c, d = m
    e, f, g, h = n
    return a * e + b * g, a * f + b * h, c * e + d * g, c * f + d * h


def minus_2(m, n):
    return tuple(i - j for i, j in zip(m, n))


def inverse_4(entry):
    block = lambda i, j: (
        entry(i, j),
        entry(i, j + 1),
        entry(i + 1, j),
        entry(i + 1, j + 1),
    )
    b, c = block(0, 2), block(2, 0)
    first = inverse_2(block(0, 0))
    first_b, c_first = times_2(first, b), times_2(c, first)
    last = inverse_2(minus_2(block(2, 2), times_2(c, first_b)))
    upper = tuple(-i for i in times_2(first_b, last))
    lower = tuple(-i for i in times_2(last, c_first))
    first = minus_2(first, times_2(upper, c_first))
    return (
        (first[0], first[1], upper[0], upper[1]),
        (first[2], first[3], upper[2], upper[3]),
        (lower[0], lower[1], last[0], last[1]),
        (lower[2], lower[3], last[2], last[3]),
    )


def inverses(m):
    lane = iota((RANK, 2 * RANK), 1)
    sub = iota((RANK, 2 * RANK), 0)
    left = lane < RANK
    place = jnp.where(left, lane, lane - RANK)
    for k in range(0, RANK, 4):
        cols = [
            jnp.where(left, m[:, k + i : k + i + 1], m[:, RANK + k + i : RANK + k + i + 1])
            for i in range(4)
        ]
        pivot = inverse_4(lambda i, j: cols[j][k + i : k + i + 1])
        rows = []
        for i in range(4):
            row = m[k + i : k + i + 1]
            for j in range(4):
                row = jnp.where(place[:1] == k + j, 1.0 if i == j else 0.0, row)
            rows.append(row)
        news = [
            (p[0] * rows[0] + p[1] * rows[1]) + (p[2] * rows[2] + p[3] * rows[3])
            for p in pivot
        ]
        m = jnp.where((place >= k) & (place < k + 4), 0.0, m)
        m = (m - cols[0] * news[0] - cols[1] * news[1]) - (
            cols[2] * news[2] + cols[3] * news[3]
        )
        for i in range(4):
            m = jnp.where(sub == k + i, news[i], m)
    return m


def score_kernel(total, held, count, cov_ref, *rest):
    peers = len(flips(count))
    grads_refs, rest = rest[:2], rest[2:]
    queries_refs, rest = rest[:peers], rest[peers:]
    out_refs, (queries, weights, sums) = rest[:4], rest[4:]
    for p in range(peers):
        queries[p] = queries_refs[p][...]
    examples = 2 * grads_refs[0].shape[1] // RANK
    half = RANK // 2
    core = lax.axis_index("tensor")
    cov = cov_ref[0]
    for p in range(1, count):
        cov = cov + cov_ref[p]
    cov = cov / total
    packed = jnp.concatenate([cov[:half, :RANK], cov[:half, RANK:]], axis=0)
    turned = packed.T
    row, col = iota((RANK, RANK), 0), iota((RANK, RANK), 1)
    cov_in = jnp.where(row >= col, packed, turned)
    cov_out = jnp.where(
        row < col, packed, jnp.where(row == col, cov[half : half + 1, :RANK], turned)
    )

    def damped(c):
        shift = 0.1 * jnp.sum(jnp.where(row == col, c, 0.0)) / RANK + 1e-06
        return jnp.where(row == col, c + shift, c)

    inverse = inverses(jnp.concatenate([damped(cov_in), damped(cov_out)], axis=1))
    inv_in, inv_out = inverse[:, :RANK], inverse[:, RANK:]
    left = jnp.concatenate(pieces(inv_out), axis=0)
    for i, piece in enumerate(pieces(inv_in)):
        weights[i] = jnp.zeros((WIDE, WIDE), BF16)
        for k in range(4):
            here = slice(k * RANK, (k + 1) * RANK)
            weights[i, here, here] = piece
    chunks = held // 4
    grads = []
    for ref in grads_refs:
        both = ref[...].astype(F32)
        for e in range(examples // 2):
            grad = both[:, e * RANK : (e + 1) * RANK]
            grads.append(jnp.concatenate([grad] * 4, axis=1))

    def of_peer(p, carry):
        u = dot(left, queries[p])
        y = u[:RANK] + (u[RANK : 2 * RANK] + u[2 * RANK :])
        high, mid, low = pieces(
            jnp.concatenate([y[:, c * WIDE : (c + 1) * WIDE] for c in range(chunks)], axis=0)
        )
        size = chunks * RANK
        by_high = dot(jnp.concatenate([high, mid, low], axis=0), weights[0])
        by_mid = dot(jnp.concatenate([high, mid], axis=0), weights[1])
        by_low = dot(high, weights[2])
        small = by_low + by_mid[size:] + by_high[2 * size :]
        precond = by_high[:size] + (by_high[size : 2 * size] + by_mid[:size] + small)
        precond = precond.astype(BF16).astype(F32)
        for e in range(examples):
            for c in range(chunks):
                sums[p, e * chunks + c : e * chunks + c + 1] = jnp.sum(
                    precond[c * RANK : (c + 1) * RANK] * grads[e], axis=0, keepdims=True
                )
        return carry

    lax.fori_loop(0, peers, of_peer, 0)
    width = 2 * held * count
    lanes = (WIDE, width)
    pick = jnp.where(iota(lanes, 0) // RANK == iota(lanes, 1) % 4, 1.0, 0.0).astype(BF16)
    flat = sums[...].reshape(peers * examples * chunks, WIDE)
    high, mid, low = pieces(flat)
    found = dot(high, pick) + (dot(mid, pick) + dot(low, pick))
    shape = (peers, examples * chunks, width)
    found = found.reshape(shape)
    lane = iota(shape, 2)
    ours = (
        (lane // (2 * held) == ((2 * iota(shape, 0)) ^ lax.axis_index("dp")))
        & ((lane // held) % 2 == core)
        & ((lane % held) // 4 == iota(shape, 1) % chunks)
    )
    found = jnp.sum(jnp.where(ours, found, 0.0), axis=0)
    scale = 1.0 / (math.sqrt(SEQ) * RANK)
    scores = [
        jnp.sum(found[e * chunks : (e + 1) * chunks], axis=0, keepdims=True) * scale
        for e in range(examples)
    ]
    share = examples // 4
    blocks = [
        jnp.concatenate(scores[i * share : (i + 1) * share], axis=0) for i in range(4)
    ]
    for i in (0, 2):
        out_refs[i][...] = jnp.where(core == 0, blocks[i], blocks[i + 1])
        out_refs[i + 1][...] = jnp.where(core == 0, blocks[i + 1], blocks[i])


def score(cov, grads, queries, total, held):
    count = cov.shape[0]
    peers = len(queries)
    examples = 2 * grads[0].shape[1] // RANK
    shape = jax.ShapeDtypeStruct((examples // 4, 2 * held * count), F32)
    return pl.pallas_call(
        functools.partial(score_kernel, total, held, count),
        out_shape=(shape,) * 4,
        cost_estimate=cost(10),
        in_specs=[VMEM] * (3 + peers),
        out_specs=(VMEM,) * 4,
        scratch_shapes=[
            pltpu.VMEM((peers,) + queries[0].shape, BF16),
            pltpu.VMEM((3, WIDE, WIDE), BF16),
            pltpu.VMEM((peers, examples * (held // 4), WIDE), F32),
        ],
        compiler_params=pltpu.CompilerParams(vmem_limit_bytes=24 * MIB),
    )(cov, *grads, *queries)


def local(train_inputs, train_grads, proj_in, proj_out, queries):
    count = lax.axis_size("dp")
    swap = [(0, 1), (1, 0)]
    held = queries.shape[0]
    spread_queries = spread(queries)
    gathered = from_peers(spread_queries, count)
    mine = project(train_inputs, train_grads, proj_in, proj_out, spread_queries)
    other = [lax.ppermute(part, "tensor", swap) for part in mine]
    cov = covariances(mine, other, [gathered[count // 4], gathered[count // 8]], count)
    cov = lax.all_to_all(cov, "dp", 0, 0, tiled=True)
    grads = gradients(mine, other)
    total = train_inputs.shape[0] * count
    pair = (grads, flipped(grads, count, 1))
    keep, to_core, to_chip, to_far = score(cov, pair, gathered, total, held)
    corner = [(i, i ^ 3) for i in range(2 * count)]
    return (
        (keep + lax.ppermute(to_core, "tensor", swap))
        + (flipped(to_chip, count, 1) + lax.ppermute(to_far, ("dp", "tensor"), corner))
    )


def solution(mesh):
    placed = (
        P(("groups", "dp"), "tensor"),
        P(("groups", "dp"), "tensor"),
        P("tensor", None),
        P("tensor", None),
        P(("groups", "dp", "tensor"), None, None),
    )
    return jax.shard_map(
        local,
        mesh=mesh,
        in_specs=placed,
        out_specs=P(("groups", "dp", "tensor"), None),
        check_vma=False,
    )
```

```python
import functools
import math

import jax
import jax.numpy as jnp
from jax import lax
from jax.experimental import pallas as pl
from jax.experimental.pallas import tpu as pltpu
from jax.sharding import PartitionSpec as P

SEQ = 64
RANK = 64
WIDE = 4 * RANK
MIB = 1 << 20
F32 = jnp.float32
BF16 = jnp.bfloat16
HBM = pl.BlockSpec(memory_space=pl.ANY)
VMEM = pl.BlockSpec(memory_space=pltpu.VMEM)


def cost(us):
    return pl.CostEstimate(flops=0, bytes_accessed=int(us * 3.7e6), transcendentals=0)


NT = (((1,), (1,)), ((), ()))


SMALL = pltpu.CompilerParams(vmem_limit_bytes=4 * MIB)


def iota(shape, dim):
    return lax.broadcasted_iota(jnp.int32, shape, dim)


def pieces(x):
    high = x.astype(BF16)
    rest = x - high.astype(F32)
    mid = rest.astype(BF16)
    low = (rest - mid.astype(F32)).astype(BF16)
    return high, mid, low


def dot(a, b):
    return jnp.dot(a, b, preferred_element_type=F32)


def spread_kernel(q_ref, out_ref):
    for k in range(q_ref.shape[0]):
        out_ref[:, k * RANK : (k + 1) * RANK] = q_ref[k]


def spread(queries):
    return pl.pallas_call(
        spread_kernel,
        out_shape=jax.ShapeDtypeStruct((RANK, queries.shape[0] * RANK), BF16),
        cost_estimate=cost(2),
        in_specs=[VMEM],
        out_specs=VMEM,
        compiler_params=SMALL,
    )(queries)


def flips(count):
    return list(range(0, count, 2))


def flipped(x, count, flip):
    return lax.ppermute(x, "dp", [(i, i ^ flip) for i in range(count)])


def from_peers(mine, count):
    known = {0: mine}
    bits = []
    while 2 << len(bits) < count:
        bits.append(2 << len(bits))
    for bit in reversed(bits[-2:]):
        known[bit] = flipped(mine, count, bit)
    for i, bit in enumerate(reversed(bits)):
        for m in sorted(known):
            if m & bit == 0 and m | bit not in known and m % (2 * bit) == 0:
                known[m | bit] = flipped(known[m], count, bit)
    return [known[m] for m in flips(count)]


def project_kernel(
    x_ref, g_ref, pin_ref, pout_ref, after_ref, first_ref, second_ref, *scratch
):
    sides = (
        (x_ref, pin_ref) + scratch[:4],
        (g_ref, pout_ref) + scratch[4:8],
    )

    def copies(side, i):
        source, factor, held, held_factor, _, sems = side
        size = source.shape[1] // sems.shape[0]
        here = pl.ds(pl.multiple_of(i * size, size), size)
        return pltpu.make_async_copy(source.at[:, here], held.at[:, here], sems.at[i])

    factors = [
        pltpu.make_async_copy(side[1], side[3], scratch[8].at[i])
        for i, side in enumerate(sides)
    ]
    for side, factor in zip(sides, factors):
        factor.start()
        for i in range(side[5].shape[0]):
            copies(side, i).start()
    for side, factor in zip(sides, factors):
        _, _, held, held_factor, total, sems = side
        size = held.shape[1] // sems.shape[0]
        total[...] = jnp.zeros_like(total)
        factor.wait()

        def block(i, carry):
            copies(side, i).wait()
            here = pl.ds(pl.multiple_of(i * size, size), size)
            total[...] += lax.dot_general(
                held[:, here], held_factor[:, here], NT, preferred_element_type=F32
            )
            return carry

        lax.fori_loop(0, sems.shape[0], block, 0)
    half = first_ref.shape[0]
    for part, out_ref in enumerate((first_ref, second_ref)):
        for i, side in enumerate(sides):
            out_ref[:, i * RANK : (i + 1) * RANK] = side[4][part * half : (part + 1) * half]


def project(train_inputs, train_grads, proj_in, proj_out, after):
    tokens = train_inputs.shape[0]
    half = jax.ShapeDtypeStruct((tokens // 2, 2 * RANK), F32)
    scratch = []
    for source, factor, blocks in (
        (train_inputs, proj_in, 2),
        (train_grads, proj_out, 4),
    ):
        scratch += [
            pltpu.VMEM(source.shape, BF16),
            pltpu.VMEM(factor.shape[::-1], BF16),
            pltpu.VMEM((tokens, RANK), F32),
            pltpu.SemaphoreType.DMA((blocks,)),
        ]
    return pl.pallas_call(
        project_kernel,
        out_shape=(half, half),
        cost_estimate=cost(8),
        in_specs=[HBM] * 5,
        out_specs=(VMEM, VMEM),
        scratch_shapes=scratch + [pltpu.SemaphoreType.DMA((2,))],
        compiler_params=pltpu.CompilerParams(vmem_limit_bytes=107 * MIB // 2),
    )(train_inputs, train_grads, proj_in.T, proj_out.T, after)


def over_rows(a):
    return lax.dot_general(
        a,
        a,
        (((0,), (0,)), ((), ())),
        precision=lax.Precision.HIGHEST,
        preferred_element_type=F32,
    )


def both_halves(refs):
    a, b, c, d = refs
    return jnp.concatenate([a[...] + c[...], b[...] + d[...]], axis=0)


def covariance_kernel(count, *refs):
    cov_ref = refs[-1]
    gram = over_rows(both_halves(refs[:4]))
    cov_in = gram[:RANK, :RANK]
    cov_out = gram[RANK:, RANK:]
    row, col = iota((RANK, RANK), 0), iota((RANK, RANK), 1)
    packed = jnp.where(row >= col, cov_in, cov_out)
    diagonal = jnp.sum(jnp.where(row == col, cov_out, 0.0), axis=0, keepdims=True)
    half = RANK // 2
    body = jnp.concatenate([packed[:half], packed[half:]], axis=1)
    tail = jnp.concatenate([jnp.broadcast_to(diagonal, (8, RANK))] * 2, axis=1)
    for p in range(count):
        cov_ref[p, :half] = body
        cov_ref[p, half:] = tail


def covariances(mine, other, after, count):
    return pl.pallas_call(
        functools.partial(covariance_kernel, count),
        out_shape=jax.ShapeDtypeStruct((count, RANK // 2 + 8, 2 * RANK), F32),
        cost_estimate=cost(2),
        in_specs=[VMEM] * (4 + len(after)),
        out_specs=VMEM,
        compiler_params=SMALL,
    )(*mine, *other, *after)


def gradient_kernel(*refs):
    grads_ref = refs[-1]
    full = both_halves(refs[:4])
    for e in range(full.shape[0] // SEQ):
        gram = over_rows(full[e * SEQ : (e + 1) * SEQ])
        grads_ref[:, e * RANK : (e + 1) * RANK] = gram[RANK:, :RANK].astype(BF16)


def gradients(mine, other):
    examples = 2 * mine[0].shape[0] // SEQ
    return pl.pallas_call(
        gradient_kernel,
        out_shape=jax.ShapeDtypeStruct((RANK, examples * RANK), BF16),
        cost_estimate=cost(2),
        in_specs=[VMEM] * 4,
        out_specs=VMEM,
        compiler_params=SMALL,
    )(*mine, *other)


def inverse_2(m):
    a, b, c, d = m
    scale = 1.0 / (a * d - b * c)
    return d * scale, -b * scale, -c * scale, a * scale


def times_2(m, n):
    a, b, c, d = m
    e, f, g, h = n
    return a * e + b * g, a * f + b * h, c * e + d * g, c * f + d * h


def minus_2(m, n):
    return tuple(i - j for i, j in zip(m, n))


def inverse_4(entry):
    block = lambda i, j: (
        entry(i, j),
        entry(i, j + 1),
        entry(i + 1, j),
        entry(i + 1, j + 1),
    )
    b, c = block(0, 2), block(2, 0)
    first = inverse_2(block(0, 0))
    first_b, c_first = times_2(first, b), times_2(c, first)
    last = inverse_2(minus_2(block(2, 2), times_2(c, first_b)))
    upper = tuple(-i for i in times_2(first_b, last))
    lower = tuple(-i for i in times_2(last, c_first))
    first = minus_2(first, times_2(upper, c_first))
    return (
        (first[0], first[1], upper[0], upper[1]),
        (first[2], first[3], upper[2], upper[3]),
        (lower[0], lower[1], last[0], last[1]),
        (lower[2], lower[3], last[2], last[3]),
    )


def with_rows(m, k, rows):
    base = k // 8 * 8
    group = m[base : base + 8]
    sub = iota(group.shape, 0)
    for i, row in enumerate(rows):
        group = jnp.where(sub == k - base + i, row, group)
    parts = [m[:base], group, m[base + 8 :]]
    return jnp.concatenate([p for p in parts if p.shape[0]], axis=0)


def inverses(m):
    lane = iota((RANK, 2 * RANK), 1)
    left = lane < RANK
    place = jnp.where(left, lane, lane - RANK)

    def columns(k):
        return [
            jnp.where(left, m[:, k + i : k + i + 1], m[:, RANK + k + i : RANK + k + i + 1])
            for i in range(4)
        ]

    def combine(weights, rows):
        return [
            (w[0] * rows[0] + w[1] * rows[1]) + (w[2] * rows[2] + w[3] * rows[3])
            for w in weights
        ]

    def update(a, cols, news, k):
        a = (a - cols[0] * news[0] - cols[1] * news[1]) - (
            cols[2] * news[2] + cols[3] * news[3]
        )
        return with_rows(a, k, news)

    cols = columns(0)
    for k in range(0, RANK, 4):
        later = columns(k + 4) if k + 4 < RANK else []
        pivot = inverse_4(lambda i, j: cols[j][k + i : k + i + 1])
        rows = []
        for i in range(4):
            row = m[k + i : k + i + 1]
            for j in range(4):
                row = jnp.where(place[:1] == k + j, 1.0 if i == j else 0.0, row)
            rows.append(row)
        cleared = jnp.where((place >= k) & (place < k + 4), 0.0, m)
        m = update(cleared, cols, combine(pivot, rows), k)
        cols = [
            update(a, cols, combine(pivot, [a[k + i : k + i + 1] for i in range(4)]), k)
            for a in later
        ]
    return m


def invert_kernel(total, cov_ref, left_ref, right_ref):
    count = cov_ref.shape[0]
    half = RANK // 2
    cov = cov_ref[0]
    for p in range(1, count):
        cov = cov + cov_ref[p]
    cov = cov / total
    packed = jnp.concatenate([cov[:half, :RANK], cov[:half, RANK:]], axis=0)
    turned = packed.T
    row, col = iota((RANK, RANK), 0), iota((RANK, RANK), 1)
    cov_in = jnp.where(row >= col, packed, turned)
    cov_out = jnp.where(
        row < col, packed, jnp.where(row == col, cov[half : half + 1, :RANK], turned)
    )

    def damped(c):
        shift = 0.1 * jnp.sum(jnp.where(row == col, c, 0.0)) / RANK + 1e-06
        return jnp.where(row == col, c + shift, c)

    inverse = inverses(jnp.concatenate([damped(cov_in), damped(cov_out)], axis=1))
    inv_in, inv_out = inverse[:, :RANK], inverse[:, RANK:]
    left_ref[...] = jnp.concatenate(pieces(inv_out), axis=0)
    for i, piece in enumerate(pieces(inv_in)):
        right_ref[i] = jnp.zeros((WIDE, WIDE), BF16)
        for k in range(4):
            here = slice(k * RANK, (k + 1) * RANK)
            right_ref[i, here, here] = piece


def invert(cov, total):
    return pl.pallas_call(
        functools.partial(invert_kernel, total),
        out_shape=(
            jax.ShapeDtypeStruct((3 * RANK, RANK), BF16),
            jax.ShapeDtypeStruct((3, WIDE, WIDE), BF16),
        ),
        cost_estimate=cost(4),
        in_specs=[VMEM],
        out_specs=(VMEM, VMEM),
        compiler_params=SMALL,
    )(cov)


def score_kernel(held, count, left_ref, weights, *rest):
    peers = len(flips(count))
    grads_refs, rest = rest[:2], rest[2:]
    queries_refs, rest = rest[:peers], rest[peers:]
    out_refs, (queries, sums) = rest[:4], rest[4:]
    for p in range(peers):
        queries[p] = queries_refs[p][...]
    examples = 2 * grads_refs[0].shape[1] // RANK
    core = lax.axis_index("tensor")
    left = left_ref[...]
    chunks = held // 4
    grads = []
    for ref in grads_refs:
        both = ref[...].astype(F32)
        for e in range(examples // 2):
            grad = both[:, e * RANK : (e + 1) * RANK]
            grads.append(jnp.concatenate([grad] * 4, axis=1))

    def of_peer(p, carry):
        u = dot(left, queries[p])
        y = u[:RANK] + (u[RANK : 2 * RANK] + u[2 * RANK :])
        high, mid, low = pieces(
            jnp.concatenate([y[:, c * WIDE : (c + 1) * WIDE] for c in range(chunks)], axis=0)
        )
        size = chunks * RANK
        by_high = dot(jnp.concatenate([high, mid, low], axis=0), weights[0])
        by_mid = dot(jnp.concatenate([high, mid], axis=0), weights[1])
        by_low = dot(high, weights[2])
        small = by_low + by_mid[size:] + by_high[2 * size :]
        precond = by_high[:size] + (by_high[size : 2 * size] + by_mid[:size] + small)
        precond = precond.astype(BF16).astype(F32)
        for e in range(examples):
            for c in range(chunks):
                sums[p, e * chunks + c : e * chunks + c + 1] = jnp.sum(
                    precond[c * RANK : (c + 1) * RANK] * grads[e], axis=0, keepdims=True
                )
        return carry

    lax.fori_loop(0, peers, of_peer, 0)
    width = 2 * held * count
    lanes = (WIDE, width)
    pick = jnp.where(iota(lanes, 0) // RANK == iota(lanes, 1) % 4, 1.0, 0.0).astype(BF16)
    flat = sums[...].reshape(peers * examples * chunks, WIDE)
    high, mid, low = pieces(flat)
    found = dot(high, pick) + (dot(mid, pick) + dot(low, pick))
    shape = (peers, examples * chunks, width)
    found = found.reshape(shape)
    lane = iota(shape, 2)
    ours = (
        (lane // (2 * held) == ((2 * iota(shape, 0)) ^ lax.axis_index("dp")))
        & ((lane // held) % 2 == core)
        & ((lane % held) // 4 == iota(shape, 1) % chunks)
    )
    found = jnp.sum(jnp.where(ours, found, 0.0), axis=0)
    scale = 1.0 / (math.sqrt(SEQ) * RANK)
    scores = [
        jnp.sum(found[e * chunks : (e + 1) * chunks], axis=0, keepdims=True) * scale
        for e in range(examples)
    ]
    share = examples // 4
    blocks = [
        jnp.concatenate(scores[i * share : (i + 1) * share], axis=0) for i in range(4)
    ]
    for i in (0, 2):
        out_refs[i][...] = jnp.where(core == 0, blocks[i], blocks[i + 1])
        out_refs[i + 1][...] = jnp.where(core == 0, blocks[i + 1], blocks[i])


def score(left, right, grads, queries, held, count):
    peers = len(queries)
    examples = 2 * grads[0].shape[1] // RANK
    shape = jax.ShapeDtypeStruct((examples // 4, 2 * held * count), F32)
    return pl.pallas_call(
        functools.partial(score_kernel, held, count),
        out_shape=(shape,) * 4,
        cost_estimate=cost(4),
        in_specs=[VMEM] * (4 + peers),
        out_specs=(VMEM,) * 4,
        scratch_shapes=[
            pltpu.VMEM((peers,) + queries[0].shape, BF16),
            pltpu.VMEM((peers, examples * (held // 4), WIDE), F32),
        ],
        compiler_params=pltpu.CompilerParams(vmem_limit_bytes=24 * MIB),
    )(left, right, *grads, *queries)


def local(train_inputs, train_grads, proj_in, proj_out, queries):
    count = lax.axis_size("dp")
    swap = [(0, 1), (1, 0)]
    held = queries.shape[0]
    spread_queries = spread(queries)
    gathered = from_peers(spread_queries, count)
    mine = project(train_inputs, train_grads, proj_in, proj_out, spread_queries)
    other = [lax.ppermute(part, "tensor", swap) for part in mine]
    cov = covariances(mine, other, [gathered[count // 4], gathered[count // 8]], count)
    cov = lax.all_to_all(cov, "dp", 0, 0, tiled=True)
    grads = gradients(mine, other)
    total = train_inputs.shape[0] * count
    pair = (grads, flipped(grads, count, 1))
    keep, to_core, to_chip, to_far = score(
        *invert(cov, total), pair, gathered, held, count
    )
    corner = [(i, i ^ 3) for i in range(2 * count)]
    return (
        (keep + lax.ppermute(to_core, "tensor", swap))
        + (flipped(to_chip, count, 1) + lax.ppermute(to_far, ("dp", "tensor"), corner))
    )


def solution(mesh):
    placed = (
        P(("groups", "dp"), "tensor"),
        P(("groups", "dp"), "tensor"),
        P("tensor", None),
        P("tensor", None),
        P(("groups", "dp", "tensor"), None, None),
    )
    return jax.shard_map(
        local,
        mesh=mesh,
        in_specs=placed,
        out_specs=P(("groups", "dp", "tensor"), None),
        check_vma=False,
    )
```

```python
import functools
import math

import jax
import jax.numpy as jnp
from jax import lax
from jax.experimental import pallas as pl
from jax.experimental.pallas import tpu as pltpu
from jax.sharding import PartitionSpec as P

SEQ = 64
RANK = 64
WIDE = 4 * RANK
MIB = 1 << 20
F32 = jnp.float32
BF16 = jnp.bfloat16
HBM = pl.BlockSpec(memory_space=pl.ANY)
VMEM = pl.BlockSpec(memory_space=pltpu.VMEM)


def cost(us):
    return pl.CostEstimate(flops=0, bytes_accessed=int(us * 3.7e6), transcendentals=0)


NT = (((1,), (1,)), ((), ()))


SMALL = pltpu.CompilerParams(vmem_limit_bytes=4 * MIB)


def iota(shape, dim):
    return lax.broadcasted_iota(jnp.int32, shape, dim)


def pieces(x):
    high = x.astype(BF16)
    rest = x - high.astype(F32)
    mid = rest.astype(BF16)
    low = (rest - mid.astype(F32)).astype(BF16)
    return high, mid, low


def dot(a, b):
    return jnp.dot(a, b, preferred_element_type=F32)


def spread_kernel(q_ref, out_ref):
    for k in range(q_ref.shape[0]):
        out_ref[:, k * RANK : (k + 1) * RANK] = q_ref[k]


def spread(queries):
    return pl.pallas_call(
        spread_kernel,
        out_shape=jax.ShapeDtypeStruct((RANK, queries.shape[0] * RANK), BF16),
        cost_estimate=cost(2),
        in_specs=[VMEM],
        out_specs=VMEM,
        compiler_params=SMALL,
    )(queries)


def flips(count):
    return list(range(0, count, 2))


def flipped(x, count, flip):
    return lax.ppermute(x, "dp", [(i, i ^ flip) for i in range(count)])


def first_from_peers(mine, count):
    known = {0: mine}
    for bit in sorted(flips(count))[1:]:
        if bit & (bit - 1) == 0 and bit * 8 > count:
            known[bit] = flipped(mine, count, bit)
    return known


def all_from_peers(known, count):
    known = dict(known)
    bit = count // 2
    while bit > 1:
        for m in sorted(known):
            if m % (2 * bit) == 0 and m | bit not in known:
                known[m | bit] = flipped(known[m], count, bit)
        bit //= 2
    return [known[m] for m in flips(count)]


def project_kernel(
    x_ref, g_ref, pin_ref, pout_ref, after_ref, first_ref, second_ref, *scratch
):
    sides = (
        (x_ref, pin_ref) + scratch[:4],
        (g_ref, pout_ref) + scratch[4:8],
    )

    def copies(side, i):
        source, factor, held, held_factor, _, sems = side
        size = source.shape[1] // sems.shape[0]
        here = pl.ds(pl.multiple_of(i * size, size), size)
        return pltpu.make_async_copy(source.at[:, here], held.at[:, here], sems.at[i])

    factors = [
        pltpu.make_async_copy(side[1], side[3], scratch[8].at[i])
        for i, side in enumerate(sides)
    ]
    for side, factor in zip(sides, factors):
        factor.start()
        for i in range(side[5].shape[0]):
            copies(side, i).start()
    for side, factor in zip(sides, factors):
        _, _, held, held_factor, total, sems = side
        size = held.shape[1] // sems.shape[0]
        total[...] = jnp.zeros_like(total)
        factor.wait()

        def block(i, carry):
            copies(side, i).wait()
            here = pl.ds(pl.multiple_of(i * size, size), size)
            total[...] += lax.dot_general(
                held[:, here], held_factor[:, here], NT, preferred_element_type=F32
            )
            return carry

        lax.fori_loop(0, sems.shape[0], block, 0)
    half = first_ref.shape[0]
    for part, out_ref in enumerate((first_ref, second_ref)):
        for i, side in enumerate(sides):
            out_ref[:, i * RANK : (i + 1) * RANK] = side[4][part * half : (part + 1) * half]


def project(train_inputs, train_grads, proj_in, proj_out, after):
    tokens = train_inputs.shape[0]
    half = jax.ShapeDtypeStruct((tokens // 2, 2 * RANK), F32)
    scratch = []
    for source, factor, blocks in (
        (train_inputs, proj_in, 2),
        (train_grads, proj_out, 4),
    ):
        scratch += [
            pltpu.VMEM(source.shape, BF16),
            pltpu.VMEM(factor.shape[::-1], BF16),
            pltpu.VMEM((tokens, RANK), F32),
            pltpu.SemaphoreType.DMA((blocks,)),
        ]
    return pl.pallas_call(
        project_kernel,
        out_shape=(half, half),
        cost_estimate=cost(8),
        in_specs=[HBM] * 5,
        out_specs=(VMEM, VMEM),
        scratch_shapes=scratch + [pltpu.SemaphoreType.DMA((2,))],
        compiler_params=pltpu.CompilerParams(vmem_limit_bytes=107 * MIB // 2),
    )(train_inputs, train_grads, proj_in.T, proj_out.T, after)


def over_rows(a):
    return lax.dot_general(
        a,
        a,
        (((0,), (0,)), ((), ())),
        precision=lax.Precision.HIGHEST,
        preferred_element_type=F32,
    )


def both_halves(refs):
    a, b, c, d = refs
    return jnp.concatenate([a[...] + c[...], b[...] + d[...]], axis=0)


def gram_kernel(early, *refs):
    cov_ref, grads_ref = refs[4 + early : 6 + early]
    full = both_halves(refs[:4])
    gram = None
    for e in range(full.shape[0] // SEQ):
        term = over_rows(full[e * SEQ : (e + 1) * SEQ])
        grads_ref[:, e * RANK : (e + 1) * RANK] = term[RANK:, :RANK].astype(BF16)
        gram = term if gram is None else gram + term
    cov_in = gram[:RANK, :RANK]
    cov_out = gram[RANK:, RANK:]
    row, col = iota((RANK, RANK), 0), iota((RANK, RANK), 1)
    packed = jnp.where(row >= col, cov_in, cov_out)
    diagonal = jnp.sum(jnp.where(row == col, cov_out, 0.0), axis=0, keepdims=True)
    half = RANK // 2
    body = jnp.concatenate([packed[:half], packed[half:]], axis=1)
    tail = jnp.concatenate([jnp.broadcast_to(diagonal, (8, RANK))] * 2, axis=1)
    cov_ref[:half] = body
    cov_ref[half:] = tail


def grams(mine, other, early):
    examples = 2 * mine[0].shape[0] // SEQ
    return pl.pallas_call(
        functools.partial(gram_kernel, len(early)),
        out_shape=[
            jax.ShapeDtypeStruct((RANK // 2 + 8, 2 * RANK), F32),
            jax.ShapeDtypeStruct((RANK, examples * RANK), BF16),
        ]
        + [jax.ShapeDtypeStruct(a.shape, a.dtype) for a in early],
        cost_estimate=cost(1),
        in_specs=[VMEM] * 4 + [HBM] * len(early),
        out_specs=[VMEM] * 2 + [HBM] * len(early),
        input_output_aliases={4 + i: 2 + i for i in range(len(early))},
        compiler_params=SMALL,
    )(*mine, *other, *early)


def inverse_2(m):
    a, b, c, d = m
    scale = 1.0 / (a * d - b * c)
    return d * scale, -b * scale, -c * scale, a * scale


def times_2(m, n):
    a, b, c, d = m
    e, f, g, h = n
    return a * e + b * g, a * f + b * h, c * e + d * g, c * f + d * h


def minus_2(m, n):
    return tuple(i - j for i, j in zip(m, n))


def inverse_4(entry):
    block = lambda i, j: (
        entry(i, j),
        entry(i, j + 1),
        entry(i + 1, j),
        entry(i + 1, j + 1),
    )
    b, c = block(0, 2), block(2, 0)
    first = inverse_2(block(0, 0))
    first_b, c_first = times_2(first, b), times_2(c, first)
    last = inverse_2(minus_2(block(2, 2), times_2(c, first_b)))
    upper = tuple(-i for i in times_2(first_b, last))
    lower = tuple(-i for i in times_2(last, c_first))
    first = minus_2(first, times_2(upper, c_first))
    return (
        (first[0], first[1], upper[0], upper[1]),
        (first[2], first[3], upper[2], upper[3]),
        (lower[0], lower[1], last[0], last[1]),
        (lower[2], lower[3], last[2], last[3]),
    )


def with_rows(m, k, rows):
    base = k // 8 * 8
    group = m[base : base + 8]
    sub = iota(group.shape, 0)
    for i, row in enumerate(rows):
        group = jnp.where(sub == k - base + i, row, group)
    parts = [m[:base], group, m[base + 8 :]]
    return jnp.concatenate([p for p in parts if p.shape[0]], axis=0)


def inverses(m):
    lane = iota((RANK, 2 * RANK), 1)
    left = lane < RANK
    place = jnp.where(left, lane, lane - RANK)

    def columns(k):
        return [
            jnp.where(left, m[:, k + i : k + i + 1], m[:, RANK + k + i : RANK + k + i + 1])
            for i in range(4)
        ]

    def combine(weights, rows):
        return [
            (w[0] * rows[0] + w[1] * rows[1]) + (w[2] * rows[2] + w[3] * rows[3])
            for w in weights
        ]

    def update(a, cols, news, k):
        a = (a - cols[0] * news[0] - cols[1] * news[1]) - (
            cols[2] * news[2] + cols[3] * news[3]
        )
        return with_rows(a, k, news)

    cols = columns(0)
    for k in range(0, RANK, 4):
        later = columns(k + 4) if k + 4 < RANK else []
        pivot = inverse_4(lambda i, j: cols[j][k + i : k + i + 1])
        rows = []
        for i in range(4):
            row = m[k + i : k + i + 1]
            for j in range(4):
                row = jnp.where(place[:1] == k + j, 1.0 if i == j else 0.0, row)
            rows.append(row)
        cleared = jnp.where((place >= k) & (place < k + 4), 0.0, m)
        m = update(cleared, cols, combine(pivot, rows), k)
        cols = [
            update(a, cols, combine(pivot, [a[k + i : k + i + 1] for i in range(4)]), k)
            for a in later
        ]
    return m


def sum_kernel(*refs):
    refs[-1][...] = functools.reduce(jnp.add, [ref[...] for ref in refs[:-1]])


def summed(arrays):
    if len(arrays) == 1:
        return arrays[0]
    return pl.pallas_call(
        sum_kernel,
        out_shape=jax.ShapeDtypeStruct(arrays[0].shape, F32),
        cost_estimate=cost(0.2),
        in_specs=[VMEM] * len(arrays),
        out_specs=VMEM,
        compiler_params=SMALL,
    )(*arrays)


def over_peers(mine, count):
    arrays = [mine]
    bit = 1
    while bit < count:
        mine = summed(arrays)
        group = [bit] if bit == 1 or 2 * bit == count else [3 * bit, 2 * bit, bit]
        arrays = [mine] + [flipped(mine, count, flip) for flip in group]
        bit *= len(group) + 1
    return arrays


def invert_kernel(total, *refs):
    left_ref, right_ref = refs[-2:]
    half = RANK // 2
    cov = functools.reduce(jnp.add, [ref[...] for ref in refs[:-2]])
    cov = cov / total
    packed = jnp.concatenate([cov[:half, :RANK], cov[:half, RANK:]], axis=0)
    turned = packed.T
    row, col = iota((RANK, RANK), 0), iota((RANK, RANK), 1)
    cov_in = jnp.where(row >= col, packed, turned)
    cov_out = jnp.where(
        row < col, packed, jnp.where(row == col, cov[half : half + 1, :RANK], turned)
    )

    def damped(c):
        shift = 0.1 * jnp.sum(jnp.where(row == col, c, 0.0)) / RANK + 1e-06
        return jnp.where(row == col, c + shift, c)

    inverse = inverses(jnp.concatenate([damped(cov_in), damped(cov_out)], axis=1))
    inv_in, inv_out = inverse[:, :RANK], inverse[:, RANK:]
    left_ref[...] = jnp.concatenate(pieces(inv_out), axis=0)
    for i, piece in enumerate(pieces(inv_in)):
        right_ref[i] = jnp.zeros((WIDE, WIDE), BF16)
        for k in range(4):
            here = slice(k * RANK, (k + 1) * RANK)
            right_ref[i, here, here] = piece


def invert(covs, total):
    return pl.pallas_call(
        functools.partial(invert_kernel, total),
        out_shape=(
            jax.ShapeDtypeStruct((3 * RANK, RANK), BF16),
            jax.ShapeDtypeStruct((3, WIDE, WIDE), BF16),
        ),
        cost_estimate=cost(4),
        in_specs=[VMEM] * len(covs),
        out_specs=(VMEM, VMEM),
        compiler_params=SMALL,
    )(*covs)


def score_kernel(held, count, left_ref, weights, *rest):
    peers = len(flips(count))
    grads_refs, rest = rest[:2], rest[2:]
    queries_refs, rest = rest[:peers], rest[peers:]
    out_refs, (queries, sums) = rest[:4], rest[4:]
    for p in range(peers):
        queries[p] = queries_refs[p][...]
    examples = 2 * grads_refs[0].shape[1] // RANK
    core = lax.axis_index("tensor")
    left = left_ref[...]
    chunks = held // 4
    grads = []
    for ref in grads_refs:
        both = ref[...].astype(F32)
        for e in range(examples // 2):
            grad = both[:, e * RANK : (e + 1) * RANK]
            grads.append(jnp.concatenate([grad] * 4, axis=1))

    def of_peer(p, carry):
        u = dot(left, queries[p])
        y = u[:RANK] + (u[RANK : 2 * RANK] + u[2 * RANK :])
        high, mid, low = pieces(
            jnp.concatenate([y[:, c * WIDE : (c + 1) * WIDE] for c in range(chunks)], axis=0)
        )
        size = chunks * RANK
        by_high = dot(jnp.concatenate([high, mid, low], axis=0), weights[0])
        by_mid = dot(jnp.concatenate([high, mid], axis=0), weights[1])
        by_low = dot(high, weights[2])
        small = by_low + by_mid[size:] + by_high[2 * size :]
        precond = by_high[:size] + (by_high[size : 2 * size] + by_mid[:size] + small)
        precond = precond.astype(BF16).astype(F32)
        for e in range(examples):
            for c in range(chunks):
                sums[p, e * chunks + c : e * chunks + c + 1] = jnp.sum(
                    precond[c * RANK : (c + 1) * RANK] * grads[e], axis=0, keepdims=True
                )
        return carry

    lax.fori_loop(0, peers, of_peer, 0, unroll=min(peers, 4))
    width = 2 * held * count
    lanes = (WIDE, width)
    pick = jnp.where(iota(lanes, 0) // RANK == iota(lanes, 1) % 4, 1.0, 0.0).astype(BF16)
    flat = sums[...].reshape(peers * examples * chunks, WIDE)
    high, mid, low = pieces(flat)
    found = dot(high, pick) + (dot(mid, pick) + dot(low, pick))
    shape = (peers, examples * chunks, width)
    found = found.reshape(shape)
    lane = iota(shape, 2)
    ours = (
        (lane // (2 * held) == ((2 * iota(shape, 0)) ^ lax.axis_index("dp")))
        & ((lane // held) % 2 == core)
        & ((lane % held) // 4 == iota(shape, 1) % chunks)
    )
    found = jnp.sum(jnp.where(ours, found, 0.0), axis=0)
    scale = 1.0 / (math.sqrt(SEQ) * RANK)
    scores = [
        jnp.sum(found[e * chunks : (e + 1) * chunks], axis=0, keepdims=True) * scale
        for e in range(examples)
    ]
    share = examples // 4
    blocks = [
        jnp.concatenate(scores[i * share : (i + 1) * share], axis=0) for i in range(4)
    ]
    for i in (0, 2):
        out_refs[i][...] = jnp.where(core == 0, blocks[i], blocks[i + 1])
        out_refs[i + 1][...] = jnp.where(core == 0, blocks[i + 1], blocks[i])


def score(left, right, grads, queries, held, count):
    peers = len(queries)
    examples = 2 * grads[0].shape[1] // RANK
    shape = jax.ShapeDtypeStruct((examples // 4, 2 * held * count), F32)
    return pl.pallas_call(
        functools.partial(score_kernel, held, count),
        out_shape=(shape,) * 4,
        cost_estimate=cost(4),
        in_specs=[VMEM] * (4 + peers),
        out_specs=(VMEM,) * 4,
        scratch_shapes=[
            pltpu.VMEM((peers,) + queries[0].shape, BF16),
            pltpu.VMEM((peers, examples * (held // 4), WIDE), F32),
        ],
        compiler_params=pltpu.CompilerParams(vmem_limit_bytes=24 * MIB),
    )(left, right, *grads, *queries)


def local(train_inputs, train_grads, proj_in, proj_out, queries):
    count = lax.axis_size("dp")
    swap = [(0, 1), (1, 0)]
    held = queries.shape[0]
    spread_queries = spread(queries)
    known = first_from_peers(spread_queries, count)
    mine = project(train_inputs, train_grads, proj_in, proj_out, spread_queries)
    other = [lax.ppermute(part, "tensor", swap) for part in mine]
    early = sorted(set(known) - {0})
    cov, grads, *arrived = grams(mine, other, [known[m] for m in early])
    known.update(zip(early, arrived))
    gathered = all_from_peers(known, count)
    covs = over_peers(cov, count)
    total = train_inputs.shape[0] * count
    pair = (grads, flipped(grads, count, 1))
    keep, to_core, to_chip, to_far = score(
        *invert(covs, total), pair, gathered, held, count
    )
    corner = [(i, i ^ 3) for i in range(2 * count)]
    return (
        (keep + lax.ppermute(to_core, "tensor", swap))
        + (flipped(to_chip, count, 1) + lax.ppermute(to_far, ("dp", "tensor"), corner))
    )


def solution(mesh):
    placed = (
        P(("groups", "dp"), "tensor"),
        P(("groups", "dp"), "tensor"),
        P("tensor", None),
        P("tensor", None),
        P(("groups", "dp", "tensor"), None, None),
    )
    return jax.shard_map(
        local,
        mesh=mesh,
        in_specs=placed,
        out_specs=P(("groups", "dp", "tensor"), None),
        check_vma=False,
    )
```

```python
import functools
import math

import jax
import jax.numpy as jnp
from jax import lax
from jax.experimental import pallas as pl
from jax.experimental.pallas import tpu as pltpu
from jax.sharding import PartitionSpec as P

SEQ = 64
RANK = 64
WIDE = 4 * RANK
MIB = 1 << 20
F32 = jnp.float32
BF16 = jnp.bfloat16
HBM = pl.BlockSpec(memory_space=pl.ANY)
VMEM = pl.BlockSpec(memory_space=pltpu.VMEM)


def cost(us):
    return pl.CostEstimate(flops=0, bytes_accessed=int(us * 3.7e6), transcendentals=0)


NT = (((1,), (1,)), ((), ()))


SMALL = pltpu.CompilerParams(vmem_limit_bytes=4 * MIB)


def iota(shape, dim):
    return lax.broadcasted_iota(jnp.int32, shape, dim)


def pieces(x):
    high = x.astype(BF16)
    rest = x - high.astype(F32)
    mid = rest.astype(BF16)
    low = (rest - mid.astype(F32)).astype(BF16)
    return high, mid, low


def dot(a, b):
    return jnp.dot(a, b, preferred_element_type=F32)


def spread_kernel(q_ref, out_ref):
    for k in range(q_ref.shape[0]):
        out_ref[:, k * RANK : (k + 1) * RANK] = q_ref[k]


def spread(queries):
    return pl.pallas_call(
        spread_kernel,
        out_shape=jax.ShapeDtypeStruct((RANK, queries.shape[0] * RANK), BF16),
        cost_estimate=cost(2),
        in_specs=[VMEM],
        out_specs=VMEM,
        compiler_params=SMALL,
    )(queries)


def flips(count):
    return list(range(0, count, 2))


def flipped(x, count, flip):
    return lax.ppermute(x, "dp", [(i, i ^ flip) for i in range(count)])


def first_from_peers(mine, count):
    known = {0: mine}
    for bit in sorted(flips(count))[1:]:
        if bit & (bit - 1) == 0 and bit * 8 > count:
            known[bit] = flipped(mine, count, bit)
    return known


def all_from_peers(known, count):
    known = dict(known)
    bit = count // 2
    while bit > 1:
        for m in sorted(known):
            if m % (2 * bit) == 0 and m | bit not in known:
                known[m | bit] = flipped(known[m], count, bit)
        bit //= 2
    return [known[m] for m in flips(count)]


def project_kernel(
    x_ref, g_ref, pin_ref, pout_ref, after_ref, first_ref, second_ref, *scratch
):
    sides = (
        (g_ref, pout_ref) + scratch[4:8],
        (x_ref, pin_ref) + scratch[:4],
    )

    def copies(side, i):
        source, factor, held, held_factor, _, sems = side
        size = source.shape[1] // sems.shape[0]
        here = pl.ds(pl.multiple_of(i * size, size), size)
        return pltpu.make_async_copy(source.at[:, here], held.at[:, here], sems.at[i])

    factors = [
        pltpu.make_async_copy(side[1], side[3], scratch[8].at[i])
        for i, side in enumerate(sides)
    ]
    for side, factor in zip(sides, factors):
        factor.start()
        for i in range(side[5].shape[0]):
            copies(side, i).start()
    for side, factor in zip(sides, factors):
        _, _, held, held_factor, total, sems = side
        size = held.shape[1] // sems.shape[0]
        total[...] = jnp.zeros_like(total)
        factor.wait()

        def block(i, carry):
            copies(side, i).wait()
            here = pl.ds(pl.multiple_of(i * size, size), size)
            total[...] += lax.dot_general(
                held[:, here], held_factor[:, here], NT, preferred_element_type=F32
            )
            return carry

        lax.fori_loop(0, sems.shape[0], block, 0)
    half = first_ref.shape[0]
    for part, out_ref in enumerate((first_ref, second_ref)):
        for i, side in enumerate(sides[::-1]):
            out_ref[:, i * RANK : (i + 1) * RANK] = side[4][part * half : (part + 1) * half]


def project(train_inputs, train_grads, proj_in, proj_out, after):
    tokens = train_inputs.shape[0]
    half = jax.ShapeDtypeStruct((tokens // 2, 2 * RANK), F32)
    scratch = []
    for source, factor, blocks in (
        (train_inputs, proj_in, 1),
        (train_grads, proj_out, 2),
    ):
        scratch += [
            pltpu.VMEM(source.shape, BF16),
            pltpu.VMEM(factor.shape[::-1], BF16),
            pltpu.VMEM((tokens, RANK), F32),
            pltpu.SemaphoreType.DMA((blocks,)),
        ]
    return pl.pallas_call(
        project_kernel,
        out_shape=(half, half),
        cost_estimate=cost(8),
        in_specs=[HBM] * 5,
        out_specs=(VMEM, VMEM),
        scratch_shapes=scratch + [pltpu.SemaphoreType.DMA((2,))],
        compiler_params=pltpu.CompilerParams(vmem_limit_bytes=107 * MIB // 2),
    )(train_inputs, train_grads, proj_in.T, proj_out.T, after)


def over_rows(a):
    return lax.dot_general(
        a,
        a,
        (((0,), (0,)), ((), ())),
        precision=lax.Precision.HIGHEST,
        preferred_element_type=F32,
    )


def both_halves(refs):
    a, b, c, d = refs
    return jnp.concatenate([a[...] + c[...], b[...] + d[...]], axis=0)


def gram_kernel(early, *refs):
    cov_ref, grads_ref = refs[4 + early : 6 + early]
    full = both_halves(refs[:4])
    gram = None
    for e in range(full.shape[0] // SEQ):
        term = over_rows(full[e * SEQ : (e + 1) * SEQ])
        grads_ref[:, e * RANK : (e + 1) * RANK] = term[RANK:, :RANK].astype(BF16)
        gram = term if gram is None else gram + term
    cov_in = gram[:RANK, :RANK]
    cov_out = gram[RANK:, RANK:]
    row, col = iota((RANK, RANK), 0), iota((RANK, RANK), 1)
    packed = jnp.where(row >= col, cov_in, cov_out)
    diagonal = jnp.sum(jnp.where(row == col, cov_out, 0.0), axis=0, keepdims=True)
    half = RANK // 2
    body = jnp.concatenate([packed[:half], packed[half:]], axis=1)
    tail = jnp.concatenate([jnp.broadcast_to(diagonal, (8, RANK))] * 2, axis=1)
    cov_ref[:half] = body
    cov_ref[half:] = tail


def grams(mine, other, early):
    examples = 2 * mine[0].shape[0] // SEQ
    return pl.pallas_call(
        functools.partial(gram_kernel, len(early)),
        out_shape=[
            jax.ShapeDtypeStruct((RANK // 2 + 8, 2 * RANK), F32),
            jax.ShapeDtypeStruct((RANK, examples * RANK), BF16),
        ]
        + [jax.ShapeDtypeStruct(a.shape, a.dtype) for a in early],
        cost_estimate=cost(1),
        in_specs=[VMEM] * 4 + [HBM] * len(early),
        out_specs=[VMEM] * 2 + [HBM] * len(early),
        input_output_aliases={4 + i: 2 + i for i in range(len(early))},
        compiler_params=SMALL,
    )(*mine, *other, *early)


def inverse_2(m):
    a, b, c, d = m
    scale = 1.0 / (a * d - b * c)
    return d * scale, -b * scale, -c * scale, a * scale


def times_2(m, n):
    a, b, c, d = m
    e, f, g, h = n
    return a * e + b * g, a * f + b * h, c * e + d * g, c * f + d * h


def minus_2(m, n):
    return tuple(i - j for i, j in zip(m, n))


def inverse_4(entry):
    block = lambda i, j: (
        entry(i, j),
        entry(i, j + 1),
        entry(i + 1, j),
        entry(i + 1, j + 1),
    )
    b, c = block(0, 2), block(2, 0)
    first = inverse_2(block(0, 0))
    first_b, c_first = times_2(first, b), times_2(c, first)
    last = inverse_2(minus_2(block(2, 2), times_2(c, first_b)))
    upper = tuple(-i for i in times_2(first_b, last))
    lower = tuple(-i for i in times_2(last, c_first))
    first = minus_2(first, times_2(upper, c_first))
    return (
        (first[0], first[1], upper[0], upper[1]),
        (first[2], first[3], upper[2], upper[3]),
        (lower[0], lower[1], last[0], last[1]),
        (lower[2], lower[3], last[2], last[3]),
    )


def with_rows(m, k, rows):
    base = k // 8 * 8
    group = m[base : base + 8]
    sub = iota(group.shape, 0)
    for i, row in enumerate(rows):
        group = jnp.where(sub == k - base + i, row, group)
    parts = [m[:base], group, m[base + 8 :]]
    return jnp.concatenate([p for p in parts if p.shape[0]], axis=0)


def inverses(m):
    lane = iota((RANK, 2 * RANK), 1)
    left = lane < RANK
    place = jnp.where(left, lane, lane - RANK)

    def columns(k):
        return [
            jnp.where(left, m[:, k + i : k + i + 1], m[:, RANK + k + i : RANK + k + i + 1])
            for i in range(4)
        ]

    def combine(weights, rows):
        return [
            (w[0] * rows[0] + w[1] * rows[1]) + (w[2] * rows[2] + w[3] * rows[3])
            for w in weights
        ]

    def update(a, cols, news, k):
        a = (a - cols[0] * news[0] - cols[1] * news[1]) - (
            cols[2] * news[2] + cols[3] * news[3]
        )
        return with_rows(a, k, news)

    cols = columns(0)
    for k in range(0, RANK, 4):
        later = columns(k + 4) if k + 4 < RANK else []
        pivot = inverse_4(lambda i, j: cols[j][k + i : k + i + 1])
        rows = []
        for i in range(4):
            row = m[k + i : k + i + 1]
            for j in range(4):
                row = jnp.where(place[:1] == k + j, 1.0 if i == j else 0.0, row)
            rows.append(row)
        cleared = jnp.where((place >= k) & (place < k + 4), 0.0, m)
        m = update(cleared, cols, combine(pivot, rows), k)
        cols = [
            update(a, cols, combine(pivot, [a[k + i : k + i + 1] for i in range(4)]), k)
            for a in later
        ]
    return m


def sum_kernel(*refs):
    refs[-1][...] = functools.reduce(jnp.add, [ref[...] for ref in refs[:-1]])


def summed(arrays):
    if len(arrays) == 1:
        return arrays[0]
    return pl.pallas_call(
        sum_kernel,
        out_shape=jax.ShapeDtypeStruct(arrays[0].shape, F32),
        cost_estimate=cost(0.2),
        in_specs=[VMEM] * len(arrays),
        out_specs=VMEM,
        compiler_params=SMALL,
    )(*arrays)


def over_peers(mine, count):
    arrays = [mine]
    bit = 1
    while bit < count:
        mine = summed(arrays)
        group = [bit] if bit == 1 or 2 * bit == count else [3 * bit, bit, 2 * bit]
        arrays = [mine] + [flipped(mine, count, flip) for flip in group]
        bit *= len(group) + 1
    return arrays


def invert_kernel(total, *refs):
    left_ref, right_ref = refs[-2:]
    half = RANK // 2
    cov = functools.reduce(jnp.add, [ref[...] for ref in refs[:-2]])
    cov = cov / total
    packed = jnp.concatenate([cov[:half, :RANK], cov[:half, RANK:]], axis=0)
    turned = packed.T
    row, col = iota((RANK, RANK), 0), iota((RANK, RANK), 1)
    cov_in = jnp.where(row >= col, packed, turned)
    cov_out = jnp.where(
        row < col, packed, jnp.where(row == col, cov[half : half + 1, :RANK], turned)
    )

    def damped(c):
        shift = 0.1 * jnp.sum(jnp.where(row == col, c, 0.0)) / RANK + 1e-06
        return jnp.where(row == col, c + shift, c)

    inverse = inverses(jnp.concatenate([damped(cov_in), damped(cov_out)], axis=1))
    inv_in, inv_out = inverse[:, :RANK], inverse[:, RANK:]
    left_ref[...] = jnp.concatenate(pieces(inv_out), axis=0)
    for i, piece in enumerate(pieces(inv_in)):
        right_ref[i] = jnp.zeros((WIDE, WIDE), BF16)
        for k in range(4):
            here = slice(k * RANK, (k + 1) * RANK)
            right_ref[i, here, here] = piece


def invert(covs, total):
    return pl.pallas_call(
        functools.partial(invert_kernel, total),
        out_shape=(
            jax.ShapeDtypeStruct((3 * RANK, RANK), BF16),
            jax.ShapeDtypeStruct((3, WIDE, WIDE), BF16),
        ),
        cost_estimate=cost(4),
        in_specs=[VMEM] * len(covs),
        out_specs=(VMEM, VMEM),
        compiler_params=SMALL,
    )(*covs)


def score_kernel(held, count, left_ref, weights, *rest):
    peers = len(flips(count))
    grads_refs, rest = rest[:2], rest[2:]
    queries_refs, rest = rest[:peers], rest[peers:]
    out_refs, (queries, sums) = rest[:4], rest[4:]
    for p in range(peers):
        queries[p] = queries_refs[p][...]
    examples = 2 * grads_refs[0].shape[1] // RANK
    core = lax.axis_index("tensor")
    left = left_ref[...]
    chunks = held // 4
    grads = []
    for ref in grads_refs:
        both = ref[...].astype(F32)
        for e in range(examples // 2):
            grad = both[:, e * RANK : (e + 1) * RANK]
            grads.append(jnp.concatenate([grad] * 4, axis=1))

    def of_peer(p, carry):
        u = dot(left, queries[p])
        y = u[:RANK] + (u[RANK : 2 * RANK] + u[2 * RANK :])
        high, mid, low = pieces(
            jnp.concatenate([y[:, c * WIDE : (c + 1) * WIDE] for c in range(chunks)], axis=0)
        )
        size = chunks * RANK
        by_high = dot(jnp.concatenate([high, mid, low], axis=0), weights[0])
        by_mid = dot(jnp.concatenate([high, mid], axis=0), weights[1])
        by_low = dot(high, weights[2])
        small = by_low + by_mid[size:] + by_high[2 * size :]
        precond = by_high[:size] + (by_high[size : 2 * size] + by_mid[:size] + small)
        precond = precond.astype(BF16).astype(F32)
        for e in range(examples):
            for c in range(chunks):
                sums[p, e * chunks + c : e * chunks + c + 1] = jnp.sum(
                    precond[c * RANK : (c + 1) * RANK] * grads[e], axis=0, keepdims=True
                )
        return carry

    lax.fori_loop(0, peers, of_peer, 0, unroll=min(peers, 4))
    width = 2 * held * count
    lanes = (WIDE, width)
    pick = jnp.where(iota(lanes, 0) // RANK == iota(lanes, 1) % 4, 1.0, 0.0).astype(BF16)
    flat = sums[...].reshape(peers * examples * chunks, WIDE)
    high, mid, low = pieces(flat)
    found = dot(high, pick) + (dot(mid, pick) + dot(low, pick))
    shape = (peers, examples * chunks, width)
    found = found.reshape(shape)
    lane = iota(shape, 2)
    ours = (
        (lane // (2 * held) == ((2 * iota(shape, 0)) ^ lax.axis_index("dp")))
        & ((lane // held) % 2 == core)
        & ((lane % held) // 4 == iota(shape, 1) % chunks)
    )
    found = jnp.sum(jnp.where(ours, found, 0.0), axis=0)
    scale = 1.0 / (math.sqrt(SEQ) * RANK)
    scores = [
        jnp.sum(found[e * chunks : (e + 1) * chunks], axis=0, keepdims=True) * scale
        for e in range(examples)
    ]
    share = examples // 4
    blocks = [
        jnp.concatenate(scores[i * share : (i + 1) * share], axis=0) for i in range(4)
    ]
    for i in (0, 2):
        out_refs[i][...] = jnp.where(core == 0, blocks[i], blocks[i + 1])
        out_refs[i + 1][...] = jnp.where(core == 0, blocks[i + 1], blocks[i])


def score(left, right, grads, queries, held, count):
    peers = len(queries)
    examples = 2 * grads[0].shape[1] // RANK
    shape = jax.ShapeDtypeStruct((examples // 4, 2 * held * count), F32)
    return pl.pallas_call(
        functools.partial(score_kernel, held, count),
        out_shape=(shape,) * 4,
        cost_estimate=cost(4),
        in_specs=[VMEM] * (4 + peers),
        out_specs=(VMEM,) * 4,
        scratch_shapes=[
            pltpu.VMEM((peers,) + queries[0].shape, BF16),
            pltpu.VMEM((peers, examples * (held // 4), WIDE), F32),
        ],
        compiler_params=pltpu.CompilerParams(vmem_limit_bytes=24 * MIB),
    )(left, right, *grads, *queries)


def local(train_inputs, train_grads, proj_in, proj_out, queries):
    count = lax.axis_size("dp")
    swap = [(0, 1), (1, 0)]
    held = queries.shape[0]
    spread_queries = spread(queries)
    known = first_from_peers(spread_queries, count)
    mine = project(train_inputs, train_grads, proj_in, proj_out, spread_queries)
    other = [lax.ppermute(part, "tensor", swap) for part in mine]
    early = sorted(set(known) - {0})
    cov, grads, *arrived = grams(mine, other, [known[m] for m in early])
    known.update(zip(early, arrived))
    gathered = all_from_peers(known, count)
    covs = over_peers(cov, count)
    total = train_inputs.shape[0] * count
    pair = (grads, flipped(grads, count, 1))
    keep, to_core, to_chip, to_far = score(
        *invert(covs, total), pair, gathered, held, count
    )
    corner = [(i, i ^ 3) for i in range(2 * count)]
    return (
        (keep + lax.ppermute(to_far, ("dp", "tensor"), corner))
        + (flipped(to_chip, count, 1) + lax.ppermute(to_core, "tensor", swap))
    )


def solution(mesh):
    placed = (
        P(("groups", "dp"), "tensor"),
        P(("groups", "dp"), "tensor"),
        P("tensor", None),
        P("tensor", None),
        P(("groups", "dp", "tensor"), None, None),
    )
    return jax.shard_map(
        local,
        mesh=mesh,
        in_specs=placed,
        out_specs=P(("groups", "dp", "tensor"), None),
        check_vma=False,
    )
```

```python
import functools
import math

import jax
import jax.numpy as jnp
from jax import lax
from jax.experimental import pallas as pl
from jax.experimental.pallas import tpu as pltpu
from jax.sharding import PartitionSpec as P

SEQ = 64
RANK = 64
WIDE = 4 * RANK
MIB = 1 << 20
F32 = jnp.float32
BF16 = jnp.bfloat16
HBM = pl.BlockSpec(memory_space=pl.ANY)
VMEM = pl.BlockSpec(memory_space=pltpu.VMEM)


def cost(us):
    return pl.CostEstimate(flops=0, bytes_accessed=int(us * 3.7e6), transcendentals=0)


NT = (((1,), (1,)), ((), ()))


SMALL = pltpu.CompilerParams(vmem_limit_bytes=4 * MIB)


def iota(shape, dim):
    return lax.broadcasted_iota(jnp.int32, shape, dim)


def pieces(x):
    high = x.astype(BF16)
    rest = x - high.astype(F32)
    mid = rest.astype(BF16)
    low = (rest - mid.astype(F32)).astype(BF16)
    return high, mid, low


def dot(a, b):
    return jnp.dot(a, b, preferred_element_type=F32)


def spread_kernel(q_ref, out_ref):
    for k in range(q_ref.shape[0]):
        out_ref[:, k * RANK : (k + 1) * RANK] = q_ref[k]


def spread(queries):
    return pl.pallas_call(
        spread_kernel,
        out_shape=jax.ShapeDtypeStruct((RANK, queries.shape[0] * RANK), BF16),
        cost_estimate=cost(2),
        in_specs=[VMEM],
        out_specs=VMEM,
        compiler_params=SMALL,
    )(queries)


def flips(count):
    return list(range(0, count, 2))


def flipped(x, count, flip):
    return lax.ppermute(x, "dp", [(i, i ^ flip) for i in range(count)])


def first_from_peers(mine, count):
    known = {0: mine}
    for bit in sorted(flips(count))[:0:-1]:
        if bit & (bit - 1) == 0 and bit * 8 > count:
            known[bit] = flipped(mine, count, bit)
    return known


def all_from_peers(known, count):
    known = dict(known)
    bit = count // 2
    while bit > 1:
        for m in sorted(known):
            if m % (2 * bit) == 0 and m | bit not in known:
                known[m | bit] = flipped(known[m], count, bit)
        bit //= 2
    return [known[m] for m in flips(count)]


def project_kernel(
    x_ref, g_ref, pin_ref, pout_ref, after_ref, first_ref, second_ref, *scratch
):
    sides = (
        (g_ref, pout_ref) + scratch[4:8],
        (x_ref, pin_ref) + scratch[:4],
    )

    def copies(side, i):
        source, factor, held, held_factor, _, sems = side
        size = source.shape[1] // sems.shape[0]
        here = pl.ds(pl.multiple_of(i * size, size), size)
        return pltpu.make_async_copy(source.at[:, here], held.at[:, here], sems.at[i])

    factors = [
        pltpu.make_async_copy(side[1], side[3], scratch[8].at[i])
        for i, side in enumerate(sides)
    ]
    for side, factor in zip(sides, factors):
        factor.start()
        for i in range(side[5].shape[0]):
            copies(side, i).start()
    for side, factor in zip(sides, factors):
        _, _, held, held_factor, total, sems = side
        size = held.shape[1] // sems.shape[0]
        total[...] = jnp.zeros_like(total)
        factor.wait()

        def block(i, carry):
            copies(side, i).wait()
            here = pl.ds(pl.multiple_of(i * size, size), size)
            total[...] += lax.dot_general(
                held[:, here], held_factor[:, here], NT, preferred_element_type=F32
            )
            return carry

        lax.fori_loop(0, sems.shape[0], block, 0)
    half = first_ref.shape[0]
    for part, out_ref in enumerate((first_ref, second_ref)):
        for i, side in enumerate(sides[::-1]):
            out_ref[:, i * RANK : (i + 1) * RANK] = side[4][part * half : (part + 1) * half]


def project(train_inputs, train_grads, proj_in, proj_out, after):
    tokens = train_inputs.shape[0]
    half = jax.ShapeDtypeStruct((tokens // 2, 2 * RANK), F32)
    scratch = []
    for source, factor, blocks in (
        (train_inputs, proj_in, 1),
        (train_grads, proj_out, 2),
    ):
        scratch += [
            pltpu.VMEM(source.shape, BF16),
            pltpu.VMEM(factor.shape[::-1], BF16),
            pltpu.VMEM((tokens, RANK), F32),
            pltpu.SemaphoreType.DMA((blocks,)),
        ]
    return pl.pallas_call(
        project_kernel,
        out_shape=(half, half),
        cost_estimate=cost(8),
        in_specs=[HBM] * 5,
        out_specs=(VMEM, VMEM),
        scratch_shapes=scratch + [pltpu.SemaphoreType.DMA((2,))],
        compiler_params=pltpu.CompilerParams(vmem_limit_bytes=107 * MIB // 2),
    )(train_inputs, train_grads, proj_in.T, proj_out.T, after)


def over_rows(a):
    return lax.dot_general(
        a,
        a,
        (((0,), (0,)), ((), ())),
        precision=lax.Precision.HIGHEST,
        preferred_element_type=F32,
    )


def both_halves(refs):
    a, b, c, d = refs
    return jnp.concatenate([a[...] + c[...], b[...] + d[...]], axis=0)


def gram_kernel(early, *refs):
    cov_ref, grads_ref = refs[4 + early : 6 + early]
    full = both_halves(refs[:4])
    gram = None
    for e in range(full.shape[0] // SEQ):
        term = over_rows(full[e * SEQ : (e + 1) * SEQ])
        grads_ref[:, e * RANK : (e + 1) * RANK] = term[RANK:, :RANK].astype(BF16)
        gram = term if gram is None else gram + term
    cov_in = gram[:RANK, :RANK]
    cov_out = gram[RANK:, RANK:]
    row, col = iota((RANK, RANK), 0), iota((RANK, RANK), 1)
    packed = jnp.where(row >= col, cov_in, cov_out)
    diagonal = jnp.sum(jnp.where(row == col, cov_out, 0.0), axis=0, keepdims=True)
    half = RANK // 2
    body = jnp.concatenate([packed[:half], packed[half:]], axis=1)
    tail = jnp.concatenate([jnp.broadcast_to(diagonal, (8, RANK))] * 2, axis=1)
    cov_ref[:half] = body
    cov_ref[half:] = tail


def grams(mine, other, early):
    examples = 2 * mine[0].shape[0] // SEQ
    return pl.pallas_call(
        functools.partial(gram_kernel, len(early)),
        out_shape=[
            jax.ShapeDtypeStruct((RANK // 2 + 8, 2 * RANK), F32),
            jax.ShapeDtypeStruct((RANK, examples * RANK), BF16),
        ]
        + [jax.ShapeDtypeStruct(a.shape, a.dtype) for a in early],
        cost_estimate=cost(1),
        in_specs=[VMEM] * 4 + [HBM] * len(early),
        out_specs=[VMEM] * 2 + [HBM] * len(early),
        input_output_aliases={4 + i: 2 + i for i in range(len(early))},
        compiler_params=SMALL,
    )(*mine, *other, *early)


def inverse_2(m):
    a, b, c, d = m
    scale = 1.0 / (a * d - b * c)
    return d * scale, -b * scale, -c * scale, a * scale


def times_2(m, n):
    a, b, c, d = m
    e, f, g, h = n
    return a * e + b * g, a * f + b * h, c * e + d * g, c * f + d * h


def minus_2(m, n):
    return tuple(i - j for i, j in zip(m, n))


def inverse_4(entry):
    block = lambda i, j: (
        entry(i, j),
        entry(i, j + 1),
        entry(i + 1, j),
        entry(i + 1, j + 1),
    )
    b, c = block(0, 2), block(2, 0)
    first = inverse_2(block(0, 0))
    first_b, c_first = times_2(first, b), times_2(c, first)
    last = inverse_2(minus_2(block(2, 2), times_2(c, first_b)))
    upper = tuple(-i for i in times_2(first_b, last))
    lower = tuple(-i for i in times_2(last, c_first))
    first = minus_2(first, times_2(upper, c_first))
    return (
        (first[0], first[1], upper[0], upper[1]),
        (first[2], first[3], upper[2], upper[3]),
        (lower[0], lower[1], last[0], last[1]),
        (lower[2], lower[3], last[2], last[3]),
    )


def with_rows(m, k, rows):
    base = k // 8 * 8
    group = m[base : base + 8]
    sub = iota(group.shape, 0)
    for i, row in enumerate(rows):
        group = jnp.where(sub == k - base + i, row, group)
    parts = [m[:base], group, m[base + 8 :]]
    return jnp.concatenate([p for p in parts if p.shape[0]], axis=0)


def inverses(m):
    lane = iota((RANK, 2 * RANK), 1)
    left = lane < RANK
    place = jnp.where(left, lane, lane - RANK)

    def columns(k):
        return [
            jnp.where(left, m[:, k + i : k + i + 1], m[:, RANK + k + i : RANK + k + i + 1])
            for i in range(4)
        ]

    def combine(weights, rows):
        return [
            (w[0] * rows[0] + w[1] * rows[1]) + (w[2] * rows[2] + w[3] * rows[3])
            for w in weights
        ]

    def update(a, cols, news, k):
        a = (a - cols[0] * news[0] - cols[1] * news[1]) - (
            cols[2] * news[2] + cols[3] * news[3]
        )
        return with_rows(a, k, news)

    cols = columns(0)
    for k in range(0, RANK, 4):
        later = columns(k + 4) if k + 4 < RANK else []
        pivot = inverse_4(lambda i, j: cols[j][k + i : k + i + 1])
        rows = []
        for i in range(4):
            row = m[k + i : k + i + 1]
            for j in range(4):
                row = jnp.where(place[:1] == k + j, 1.0 if i == j else 0.0, row)
            rows.append(row)
        cleared = jnp.where((place >= k) & (place < k + 4), 0.0, m)
        m = update(cleared, cols, combine(pivot, rows), k)
        cols = [
            update(a, cols, combine(pivot, [a[k + i : k + i + 1] for i in range(4)]), k)
            for a in later
        ]
    return m


def sum_kernel(*refs):
    refs[-1][...] = functools.reduce(jnp.add, [ref[...] for ref in refs[:-1]])


def summed(arrays):
    if len(arrays) == 1:
        return arrays[0]
    return pl.pallas_call(
        sum_kernel,
        out_shape=jax.ShapeDtypeStruct(arrays[0].shape, F32),
        cost_estimate=cost(0.2),
        in_specs=[VMEM] * len(arrays),
        out_specs=VMEM,
        compiler_params=SMALL,
    )(*arrays)


def over_peers(mine, count):
    groups, bit = [], 1
    while bit < count:
        groups.append([bit] if bit == 1 or 2 * bit == count else [3 * bit, bit, 2 * bit])
        bit *= len(groups[-1]) + 1
    arrays = [mine]
    for group in reversed(groups):
        mine = summed(arrays)
        arrays = [mine] + [flipped(mine, count, flip) for flip in group]
    return arrays


def invert_kernel(total, *refs):
    left_ref, right_ref = refs[-2:]
    half = RANK // 2
    cov = functools.reduce(jnp.add, [ref[...] for ref in refs[:-2]])
    cov = cov / total
    packed = jnp.concatenate([cov[:half, :RANK], cov[:half, RANK:]], axis=0)
    turned = packed.T
    row, col = iota((RANK, RANK), 0), iota((RANK, RANK), 1)
    cov_in = jnp.where(row >= col, packed, turned)
    cov_out = jnp.where(
        row < col, packed, jnp.where(row == col, cov[half : half + 1, :RANK], turned)
    )

    def damped(c):
        shift = 0.1 * jnp.sum(jnp.where(row == col, c, 0.0)) / RANK + 1e-06
        return jnp.where(row == col, c + shift, c)

    inverse = inverses(jnp.concatenate([damped(cov_in), damped(cov_out)], axis=1))
    inv_in, inv_out = inverse[:, :RANK], inverse[:, RANK:]
    left_ref[...] = jnp.concatenate(pieces(inv_out), axis=0)
    for i, piece in enumerate(pieces(inv_in)):
        right_ref[i] = jnp.zeros((WIDE, WIDE), BF16)
        for k in range(4):
            here = slice(k * RANK, (k + 1) * RANK)
            right_ref[i, here, here] = piece


def invert(covs, total):
    return pl.pallas_call(
        functools.partial(invert_kernel, total),
        out_shape=(
            jax.ShapeDtypeStruct((3 * RANK, RANK), BF16),
            jax.ShapeDtypeStruct((3, WIDE, WIDE), BF16),
        ),
        cost_estimate=cost(4),
        in_specs=[VMEM] * len(covs),
        out_specs=(VMEM, VMEM),
        compiler_params=SMALL,
    )(*covs)


def score_kernel(held, count, left_ref, weights, *rest):
    peers = len(flips(count))
    grads_refs, rest = rest[:2], rest[2:]
    queries_refs, rest = rest[:peers], rest[peers:]
    out_refs, (queries, sums) = rest[:4], rest[4:]
    for p in range(peers):
        queries[p] = queries_refs[p][...]
    examples = 2 * grads_refs[0].shape[1] // RANK
    core = lax.axis_index("tensor")
    left = left_ref[...]
    chunks = held // 4
    grads = []
    for ref in grads_refs:
        both = ref[...].astype(F32)
        for e in range(examples // 2):
            grad = both[:, e * RANK : (e + 1) * RANK]
            grads.append(jnp.concatenate([grad] * 4, axis=1))

    def of_peer(p, carry):
        u = dot(left, queries[p])
        y = u[:RANK] + (u[RANK : 2 * RANK] + u[2 * RANK :])
        high, mid, low = pieces(
            jnp.concatenate([y[:, c * WIDE : (c + 1) * WIDE] for c in range(chunks)], axis=0)
        )
        size = chunks * RANK
        by_high = dot(jnp.concatenate([high, mid, low], axis=0), weights[0])
        by_mid = dot(jnp.concatenate([high, mid], axis=0), weights[1])
        by_low = dot(high, weights[2])
        small = by_low + by_mid[size:] + by_high[2 * size :]
        precond = by_high[:size] + (by_high[size : 2 * size] + by_mid[:size] + small)
        precond = precond.astype(BF16).astype(F32)
        for e in range(examples):
            for c in range(chunks):
                sums[p, e * chunks + c : e * chunks + c + 1] = jnp.sum(
                    precond[c * RANK : (c + 1) * RANK] * grads[e], axis=0, keepdims=True
                )
        return carry

    lax.fori_loop(0, peers, of_peer, 0, unroll=min(peers, 4))
    width = 2 * held * count
    lanes = (WIDE, width)
    pick = jnp.where(iota(lanes, 0) // RANK == iota(lanes, 1) % 4, 1.0, 0.0).astype(BF16)
    flat = sums[...].reshape(peers * examples * chunks, WIDE)
    high, mid, low = pieces(flat)
    found = dot(high, pick) + (dot(mid, pick) + dot(low, pick))
    shape = (peers, examples * chunks, width)
    found = found.reshape(shape)
    lane = iota(shape, 2)
    ours = (
        (lane // (2 * held) == ((2 * iota(shape, 0)) ^ lax.axis_index("dp")))
        & ((lane // held) % 2 == core)
        & ((lane % held) // 4 == iota(shape, 1) % chunks)
    )
    found = jnp.sum(jnp.where(ours, found, 0.0), axis=0)
    scale = 1.0 / (math.sqrt(SEQ) * RANK)
    scores = [
        jnp.sum(found[e * chunks : (e + 1) * chunks], axis=0, keepdims=True) * scale
        for e in range(examples)
    ]
    share = examples // 4
    blocks = [
        jnp.concatenate(scores[i * share : (i + 1) * share], axis=0) for i in range(4)
    ]
    for i in (0, 2):
        out_refs[i][...] = jnp.where(core == 0, blocks[i], blocks[i + 1])
        out_refs[i + 1][...] = jnp.where(core == 0, blocks[i + 1], blocks[i])


def score(left, right, grads, queries, held, count):
    peers = len(queries)
    examples = 2 * grads[0].shape[1] // RANK
    shape = jax.ShapeDtypeStruct((examples // 4, 2 * held * count), F32)
    return pl.pallas_call(
        functools.partial(score_kernel, held, count),
        out_shape=(shape,) * 4,
        cost_estimate=cost(4),
        in_specs=[VMEM] * (4 + peers),
        out_specs=(VMEM,) * 4,
        scratch_shapes=[
            pltpu.VMEM((peers,) + queries[0].shape, BF16),
            pltpu.VMEM((peers, examples * (held // 4), WIDE), F32),
        ],
        compiler_params=pltpu.CompilerParams(vmem_limit_bytes=24 * MIB),
    )(left, right, *grads, *queries)


def local(train_inputs, train_grads, proj_in, proj_out, queries):
    count = lax.axis_size("dp")
    swap = [(0, 1), (1, 0)]
    held = queries.shape[0]
    spread_queries = spread(queries)
    known = first_from_peers(spread_queries, count)
    mine = project(train_inputs, train_grads, proj_in, proj_out, spread_queries)
    other = [lax.ppermute(part, "tensor", swap) for part in mine]
    early = sorted(set(known) - {0}, reverse=True)
    cov, grads, *arrived = grams(mine, other, [known[m] for m in early])
    known.update(zip(early, arrived))
    gathered = all_from_peers(known, count)
    covs = over_peers(cov, count)
    total = train_inputs.shape[0] * count
    pair = (grads, flipped(grads, count, 1))
    keep, to_core, to_chip, to_far = score(
        *invert(covs, total), pair, gathered, held, count
    )
    corner = [(i, i ^ 3) for i in range(2 * count)]
    return (
        (keep + lax.ppermute(to_far, ("dp", "tensor"), corner))
        + (flipped(to_chip, count, 1) + lax.ppermute(to_core, "tensor", swap))
    )


def solution(mesh):
    placed = (
        P(("groups", "dp"), "tensor"),
        P(("groups", "dp"), "tensor"),
        P("tensor", None),
        P("tensor", None),
        P(("groups", "dp", "tensor"), None, None),
    )
    return jax.shard_map(
        local,
        mesh=mesh,
        in_specs=placed,
        out_specs=P(("groups", "dp", "tensor"), None),
        check_vma=False,
    )
```

```python
import functools
import math

import jax
import jax.numpy as jnp
from jax import lax
from jax.experimental import pallas as pl
from jax.experimental.pallas import tpu as pltpu
from jax.sharding import PartitionSpec as P

SEQ = 64
RANK = 64
WIDE = 4 * RANK
MIB = 1 << 20
F32 = jnp.float32
BF16 = jnp.bfloat16
HBM = pl.BlockSpec(memory_space=pl.ANY)
VMEM = pl.BlockSpec(memory_space=pltpu.VMEM)


def cost(us):
    return pl.CostEstimate(flops=0, bytes_accessed=int(us * 3.7e6), transcendentals=0)


NT = (((1,), (1,)), ((), ()))


SMALL = pltpu.CompilerParams(vmem_limit_bytes=4 * MIB)


def iota(shape, dim):
    return lax.broadcasted_iota(jnp.int32, shape, dim)


def pieces(x):
    high = x.astype(BF16)
    rest = x - high.astype(F32)
    mid = rest.astype(BF16)
    low = (rest - mid.astype(F32)).astype(BF16)
    return high, mid, low


def dot(a, b):
    return jnp.dot(a, b, preferred_element_type=F32)


def spread_kernel(q_ref, out_ref):
    for k in range(q_ref.shape[0]):
        out_ref[:, k * RANK : (k + 1) * RANK] = q_ref[k]


def spread(queries):
    return pl.pallas_call(
        spread_kernel,
        out_shape=jax.ShapeDtypeStruct((RANK, queries.shape[0] * RANK), BF16),
        cost_estimate=cost(2),
        in_specs=[VMEM],
        out_specs=VMEM,
        compiler_params=SMALL,
    )(queries)


def flips(count):
    return list(range(0, count, 2))


def flipped(x, count, flip):
    return lax.ppermute(x, "dp", [(i, i ^ flip) for i in range(count)])


def first_from_peers(mine, count):
    known = {0: mine}
    for bit in sorted(flips(count))[:0:-1]:
        if bit & (bit - 1) == 0 and bit * 8 > count:
            known[bit] = flipped(mine, count, bit)
    return known


def all_from_peers(known, count):
    known = dict(known)
    bit = count // 2
    while bit > 1:
        for m in sorted(known):
            if m % (2 * bit) == 0 and m | bit not in known:
                known[m | bit] = flipped(known[m], count, bit)
        bit //= 2
    return [known[m] for m in flips(count)]


def project_kernel(
    x_ref, g_ref, pin_ref, pout_ref, after_ref, first_ref, second_ref, *scratch
):
    sides = (
        (g_ref, pout_ref) + scratch[4:8],
        (x_ref, pin_ref) + scratch[:4],
    )

    def copies(side, i):
        source, factor, held, held_factor, _, sems = side
        size = source.shape[1] // sems.shape[0]
        here = pl.ds(pl.multiple_of(i * size, size), size)
        return pltpu.make_async_copy(source.at[:, here], held.at[:, here], sems.at[i])

    factors = [
        pltpu.make_async_copy(side[1], side[3], scratch[8].at[i])
        for i, side in enumerate(sides)
    ]
    for side, factor in zip(sides, factors):
        factor.start()
        for i in range(side[5].shape[0]):
            copies(side, i).start()
    for side, factor in zip(sides, factors):
        _, _, held, held_factor, total, sems = side
        size = held.shape[1] // sems.shape[0]
        total[...] = jnp.zeros_like(total)
        factor.wait()

        def block(i, carry):
            copies(side, i).wait()
            here = pl.ds(pl.multiple_of(i * size, size), size)
            total[...] += lax.dot_general(
                held[:, here], held_factor[:, here], NT, preferred_element_type=F32
            )
            return carry

        lax.fori_loop(0, sems.shape[0], block, 0)
    half = first_ref.shape[0]
    for part, out_ref in enumerate((first_ref, second_ref)):
        for i, side in enumerate(sides[::-1]):
            out_ref[:, i * RANK : (i + 1) * RANK] = side[4][part * half : (part + 1) * half]


def project(train_inputs, train_grads, proj_in, proj_out, after):
    tokens = train_inputs.shape[0]
    half = jax.ShapeDtypeStruct((tokens // 2, 2 * RANK), F32)
    scratch = []
    for source, factor, blocks in (
        (train_inputs, proj_in, 1),
        (train_grads, proj_out, 2),
    ):
        scratch += [
            pltpu.VMEM(source.shape, BF16),
            pltpu.VMEM(factor.shape[::-1], BF16),
            pltpu.VMEM((tokens, RANK), F32),
            pltpu.SemaphoreType.DMA((blocks,)),
        ]
    return pl.pallas_call(
        project_kernel,
        out_shape=(half, half),
        cost_estimate=cost(8),
        in_specs=[HBM] * 5,
        out_specs=(VMEM, VMEM),
        scratch_shapes=scratch + [pltpu.SemaphoreType.DMA((2,))],
        compiler_params=pltpu.CompilerParams(vmem_limit_bytes=107 * MIB // 2),
    )(train_inputs, train_grads, proj_in.T, proj_out.T, after)


def over_rows(a):
    return lax.dot_general(
        a,
        a,
        (((0,), (0,)), ((), ())),
        precision=lax.Precision.HIGHEST,
        preferred_element_type=F32,
    )


def both_halves(refs):
    a, b, c, d = refs
    return jnp.concatenate([a[...] + c[...], b[...] + d[...]], axis=0)


def gram_kernel(early, *refs):
    cov_ref, grads_ref = refs[4 + early : 6 + early]
    full = both_halves(refs[:4])
    gram = None
    for e in range(full.shape[0] // SEQ):
        term = over_rows(full[e * SEQ : (e + 1) * SEQ])
        grads_ref[:, e * RANK : (e + 1) * RANK] = term[RANK:, :RANK].astype(BF16)
        gram = term if gram is None else gram + term
    cov_in = gram[:RANK, :RANK]
    cov_out = gram[RANK:, RANK:]
    row, col = iota((RANK, RANK), 0), iota((RANK, RANK), 1)
    packed = jnp.where(row >= col, cov_in, cov_out)
    diagonal = jnp.sum(jnp.where(row == col, cov_out, 0.0), axis=0, keepdims=True)
    half = RANK // 2
    body = jnp.concatenate([packed[:half], packed[half:]], axis=1)
    tail = jnp.concatenate([jnp.broadcast_to(diagonal, (8, RANK))] * 2, axis=1)
    cov_ref[:half] = body
    cov_ref[half:] = tail


def grams(mine, other, early):
    examples = 2 * mine[0].shape[0] // SEQ
    return pl.pallas_call(
        functools.partial(gram_kernel, len(early)),
        out_shape=[
            jax.ShapeDtypeStruct((RANK // 2 + 8, 2 * RANK), F32),
            jax.ShapeDtypeStruct((RANK, examples * RANK), BF16),
        ]
        + [jax.ShapeDtypeStruct(a.shape, a.dtype) for a in early],
        cost_estimate=cost(1),
        in_specs=[VMEM] * 4 + [HBM] * len(early),
        out_specs=[VMEM] * 2 + [HBM] * len(early),
        input_output_aliases={4 + i: 2 + i for i in range(len(early))},
        compiler_params=SMALL,
    )(*mine, *other, *early)


def inverse_2(m):
    a, b, c, d = m
    scale = 1.0 / (a * d - b * c)
    return d * scale, -b * scale, -c * scale, a * scale


def times_2(m, n):
    a, b, c, d = m
    e, f, g, h = n
    return a * e + b * g, a * f + b * h, c * e + d * g, c * f + d * h


def minus_2(m, n):
    return tuple(i - j for i, j in zip(m, n))


def inverse_4(entry):
    block = lambda i, j: (
        entry(i, j),
        entry(i, j + 1),
        entry(i + 1, j),
        entry(i + 1, j + 1),
    )
    b, c = block(0, 2), block(2, 0)
    first = inverse_2(block(0, 0))
    first_b, c_first = times_2(first, b), times_2(c, first)
    last = inverse_2(minus_2(block(2, 2), times_2(c, first_b)))
    upper = tuple(-i for i in times_2(first_b, last))
    lower = tuple(-i for i in times_2(last, c_first))
    first = minus_2(first, times_2(upper, c_first))
    return (
        (first[0], first[1], upper[0], upper[1]),
        (first[2], first[3], upper[2], upper[3]),
        (lower[0], lower[1], last[0], last[1]),
        (lower[2], lower[3], last[2], last[3]),
    )


def with_rows(m, k, rows):
    base = k // 8 * 8
    group = m[base : base + 8]
    sub = iota(group.shape, 0)
    for i, row in enumerate(rows):
        group = jnp.where(sub == k - base + i, row, group)
    parts = [m[:base], group, m[base + 8 :]]
    return jnp.concatenate([p for p in parts if p.shape[0]], axis=0)


def inverses(m):
    lane = iota((RANK, 2 * RANK), 1)
    left = lane < RANK
    place = jnp.where(left, lane, lane - RANK)

    def columns(k):
        return [
            jnp.where(left, m[:, k + i : k + i + 1], m[:, RANK + k + i : RANK + k + i + 1])
            for i in range(4)
        ]

    def combine(weights, rows):
        return [
            (w[0] * rows[0] + w[1] * rows[1]) + (w[2] * rows[2] + w[3] * rows[3])
            for w in weights
        ]

    def update(a, cols, news, k):
        a = (a - cols[0] * news[0] - cols[1] * news[1]) - (
            cols[2] * news[2] + cols[3] * news[3]
        )
        return with_rows(a, k, news)

    cols = columns(0)
    for k in range(0, RANK, 4):
        later = columns(k + 4) if k + 4 < RANK else []
        pivot = inverse_4(lambda i, j: cols[j][k + i : k + i + 1])
        rows = []
        for i in range(4):
            row = m[k + i : k + i + 1]
            for j in range(4):
                row = jnp.where(place[:1] == k + j, 1.0 if i == j else 0.0, row)
            rows.append(row)
        cleared = jnp.where((place >= k) & (place < k + 4), 0.0, m)
        m = update(cleared, cols, combine(pivot, rows), k)
        cols = [
            update(a, cols, combine(pivot, [a[k + i : k + i + 1] for i in range(4)]), k)
            for a in later
        ]
    return m


def sum_kernel(*refs):
    refs[-1][...] = functools.reduce(jnp.add, [ref[...] for ref in refs[:-1]])


def summed(arrays):
    if len(arrays) == 1:
        return arrays[0]
    return pl.pallas_call(
        sum_kernel,
        out_shape=jax.ShapeDtypeStruct(arrays[0].shape, F32),
        cost_estimate=cost(0.2),
        in_specs=[VMEM] * len(arrays),
        out_specs=VMEM,
        compiler_params=SMALL,
    )(*arrays)


def over_peers(mine, count):
    arrays = [mine]
    bit = 1
    while bit < count:
        mine = summed(arrays)
        group = [bit] if bit == 1 or 2 * bit == count else [3 * bit, bit, 2 * bit]
        arrays = [mine] + [flipped(mine, count, flip) for flip in group]
        bit *= len(group) + 1
    return arrays


def invert_kernel(total, *refs):
    left_ref, right_ref = refs[-2:]
    half = RANK // 2
    cov = functools.reduce(jnp.add, [ref[...] for ref in refs[:-2]])
    cov = cov / total
    packed = jnp.concatenate([cov[:half, :RANK], cov[:half, RANK:]], axis=0)
    turned = packed.T
    row, col = iota((RANK, RANK), 0), iota((RANK, RANK), 1)
    cov_in = jnp.where(row >= col, packed, turned)
    cov_out = jnp.where(
        row < col, packed, jnp.where(row == col, cov[half : half + 1, :RANK], turned)
    )

    def damped(c):
        shift = 0.1 * jnp.sum(jnp.where(row == col, c, 0.0)) / RANK + 1e-06
        return jnp.where(row == col, c + shift, c)

    inverse = inverses(jnp.concatenate([damped(cov_in), damped(cov_out)], axis=1))
    inv_in, inv_out = inverse[:, :RANK], inverse[:, RANK:]
    left_ref[...] = jnp.concatenate(pieces(inv_out), axis=0)
    for i, piece in enumerate(pieces(inv_in)):
        right_ref[i] = jnp.zeros((WIDE, WIDE), BF16)
        for k in range(4):
            here = slice(k * RANK, (k + 1) * RANK)
            right_ref[i, here, here] = piece


def invert(covs, total):
    return pl.pallas_call(
        functools.partial(invert_kernel, total),
        out_shape=(
            jax.ShapeDtypeStruct((3 * RANK, RANK), BF16),
            jax.ShapeDtypeStruct((3, WIDE, WIDE), BF16),
        ),
        cost_estimate=cost(4),
        in_specs=[VMEM] * len(covs),
        out_specs=(VMEM, VMEM),
        compiler_params=SMALL,
    )(*covs)


def score_kernel(held, count, left_ref, weights, *rest):
    peers = len(flips(count))
    grads_refs, rest = rest[:2], rest[2:]
    queries_refs, rest = rest[:peers], rest[peers:]
    out_refs, (queries, sums) = rest[:4], rest[4:]
    for p in range(peers):
        queries[p] = queries_refs[p][...]
    examples = 2 * grads_refs[0].shape[1] // RANK
    core = lax.axis_index("tensor")
    left = left_ref[...]
    chunks = held // 4
    grads = []
    for ref in grads_refs:
        both = ref[...].astype(F32)
        for e in range(examples // 2):
            grad = both[:, e * RANK : (e + 1) * RANK]
            grads.append(jnp.concatenate([grad] * 4, axis=1))

    def of_peer(p, carry):
        u = dot(left, queries[p])
        y = u[:RANK] + (u[RANK : 2 * RANK] + u[2 * RANK :])
        high, mid, low = pieces(
            jnp.concatenate([y[:, c * WIDE : (c + 1) * WIDE] for c in range(chunks)], axis=0)
        )
        size = chunks * RANK
        by_high = dot(jnp.concatenate([high, mid, low], axis=0), weights[0])
        by_mid = dot(jnp.concatenate([high, mid], axis=0), weights[1])
        by_low = dot(high, weights[2])
        small = by_low + by_mid[size:] + by_high[2 * size :]
        precond = by_high[:size] + (by_high[size : 2 * size] + by_mid[:size] + small)
        precond = precond.astype(BF16).astype(F32)
        for e in range(examples):
            for c in range(chunks):
                sums[p, e * chunks + c : e * chunks + c + 1] = jnp.sum(
                    precond[c * RANK : (c + 1) * RANK] * grads[e], axis=0, keepdims=True
                )
        return carry

    lax.fori_loop(0, peers, of_peer, 0, unroll=min(peers, 4))
    width = 2 * held * count
    lanes = (WIDE, width)
    pick = jnp.where(iota(lanes, 0) // RANK == iota(lanes, 1) % 4, 1.0, 0.0).astype(BF16)
    flat = sums[...].reshape(peers * examples * chunks, WIDE)
    high, mid, low = pieces(flat)
    found = dot(high, pick) + (dot(mid, pick) + dot(low, pick))
    shape = (peers, examples * chunks, width)
    found = found.reshape(shape)
    lane = iota(shape, 2)
    ours = (
        (lane // (2 * held) == ((2 * iota(shape, 0)) ^ lax.axis_index("dp")))
        & ((lane // held) % 2 == core)
        & ((lane % held) // 4 == iota(shape, 1) % chunks)
    )
    found = jnp.sum(jnp.where(ours, found, 0.0), axis=0)
    scale = 1.0 / (math.sqrt(SEQ) * RANK)
    scores = [
        jnp.sum(found[e * chunks : (e + 1) * chunks], axis=0, keepdims=True) * scale
        for e in range(examples)
    ]
    share = examples // 4
    blocks = [
        jnp.concatenate(scores[i * share : (i + 1) * share], axis=0) for i in range(4)
    ]
    for i in (0, 2):
        out_refs[i][...] = jnp.where(core == 0, blocks[i], blocks[i + 1])
        out_refs[i + 1][...] = jnp.where(core == 0, blocks[i + 1], blocks[i])


def score(left, right, grads, queries, held, count):
    peers = len(queries)
    examples = 2 * grads[0].shape[1] // RANK
    shape = jax.ShapeDtypeStruct((examples // 4, 2 * held * count), F32)
    return pl.pallas_call(
        functools.partial(score_kernel, held, count),
        out_shape=(shape,) * 4,
        cost_estimate=cost(4),
        in_specs=[VMEM] * (4 + peers),
        out_specs=(VMEM,) * 4,
        scratch_shapes=[
            pltpu.VMEM((peers,) + queries[0].shape, BF16),
            pltpu.VMEM((peers, examples * (held // 4), WIDE), F32),
        ],
        compiler_params=pltpu.CompilerParams(vmem_limit_bytes=24 * MIB),
    )(left, right, *grads, *queries)


def local(train_inputs, train_grads, proj_in, proj_out, queries):
    count = lax.axis_size("dp")
    swap = [(0, 1), (1, 0)]
    held = queries.shape[0]
    spread_queries = spread(queries)
    known = first_from_peers(spread_queries, count)
    mine = project(train_inputs, train_grads, proj_in, proj_out, spread_queries)
    other = [lax.ppermute(part, "tensor", swap) for part in mine]
    early = sorted(set(known) - {0}, reverse=True)
    cov, grads, *arrived = grams(mine, other, [known[m] for m in early])
    known.update(zip(early, arrived))
    gathered = all_from_peers(known, count)
    covs = over_peers(cov, count)
    total = train_inputs.shape[0] * count
    pair = (grads, flipped(grads, count, 1))
    keep, to_core, to_chip, to_far = score(
        *invert(covs, total), pair, gathered, held, count
    )
    corner = [(i, i ^ 3) for i in range(2 * count)]
    return (
        (keep + lax.ppermute(to_far, ("dp", "tensor"), corner))
        + (flipped(to_chip, count, 1) + lax.ppermute(to_core, "tensor", swap))
    )


def solution(mesh):
    placed = (
        P(("groups", "dp"), "tensor"),
        P(("groups", "dp"), "tensor"),
        P("tensor", None),
        P("tensor", None),
        P(("groups", "dp", "tensor"), None, None),
    )
    return jax.shard_map(
        local,
        mesh=mesh,
        in_specs=placed,
        out_specs=P(("groups", "dp", "tensor"), None),
        check_vma=False,
    )
```
